128 devices in a mesh: member: 4 (over z_lo, core), grid: 32 (over x, y, z_hi).
Axes of the slice: x: 4, y: 4, z: 4 (z_hi: 2, z_lo: 2; z = z_hi * 2 + z_lo), core: 2. Of those that a mesh axis runs over, the one named last changes fastest.
Arguments:
- fields: bfloat16 [32, 64, 65536], P('member', None, 'grid'), may hold values from -8 to 8
- cotangent: bfloat16 [32, 64, 65536], P('member', None, 'grid'), may hold values from -6 to 6
- w_query: bfloat16 [64, 64], replicated, may hold values from -0.75 to 0.75
- w_key: bfloat16 [64, 64], replicated, may hold values from -0.75 to 0.75
- w_value: bfloat16 [64, 64], replicated, may hold values from -0.75 to 0.75
- w_out: bfloat16 [64, 64], replicated, may hold values from -0.75 to 0.75
- w_up: bfloat16 [256, 64], replicated, may hold values from -0.75 to 0.75
- w_down: bfloat16 [64, 256], replicated, may hold values from -0.375 to 0.375
- gain_attn: float32 [64], replicated, may hold values from 0.1 to 1.9
- gain_mlp: float32 [64], replicated, may hold values from 0.1 to 1.9
Outputs:
- result: bfloat16 [32, 64, 65536], P('member', None, 'grid')
- grad_fields: bfloat16 [32, 64, 65536], P('member', None, 'grid')
- grad_w_query: float32 [64, 64], replicated
- grad_w_key: float32 [64, 64], replicated
- grad_w_value: float32 [64, 64], replicated
- grad_w_out: float32 [64, 64], replicated
- grad_w_up: float32 [256, 64], replicated
- grad_w_down: float32 [64, 256], replicated
- grad_gain_attn: float32 [64], replicated
- grad_gain_mlp: float32 [64], replicated
The draws below stay inside these ranges and needn't reach their ends.
All inputs are finite; a program needn't handle non-finite values.
Results may differ from the reference program's by a relative error of at most 0.0076.
Values may be sent and summed in bfloat16 or wider, within the bound.
No kernel may reach another device: no remote copies, remote signals or barrier semaphores. Data moves between devices by JAX's collectives and lax.ppermute only.
A program may use at most 192 MiB of HBM per device.

```python
import jax
import jax.numpy as jnp
from jax import lax

MEMBERS = 32
G_DEV = 2048
LOCATION_NUMBER = 65536
CHANNELS = 64
HEADS = 4
FEATURE_PER_PART = 16
INNER = 256


def draw_fields(key, part):
    key = jax.random.fold_in(key, 17)
    keys = jax.random.split(key, 4)
    pattern = jnp.clip(jax.random.normal(keys[0], (MEMBERS, CHANNELS, 4), jnp.float32), -3.0, 3.0)
    region_index = jnp.arange(LOCATION_NUMBER, dtype=jnp.int32) * 4 // LOCATION_NUMBER
    coherent = pattern
    rough_part = jnp.clip(jax.random.normal(keys[3], (MEMBERS, CHANNELS, LOCATION_NUMBER), jnp.float32), -3.0, 3.0)
    return (coherent[:, :, region_index] + rough_part).astype(jnp.bfloat16)


def steps_of(own_key, extent, shards, least, high):
    level, own = 1.0, jax.random.fold_in(own_key, 6)
    for dim, blocks in shards:
        heights = jnp.exp(jax.random.uniform(jax.random.fold_in(own, dim), (blocks,), jnp.float32, least / len(shards), high / len(shards)))
        level = level * jnp.repeat(heights, extent[dim] // blocks).reshape([-1 if axis == dim else 1 for axis in range(len(extent))])
    return level


def gaussian(rng, dims, deviation, bound, shards=(), held_as=jnp.bfloat16):
    loudness = steps_of(rng, dims, shards, -0.22, 0.18) if shards else 1.0
    entries = jax.random.normal(rng, dims, jnp.float32) * deviation * loudness
    return jnp.minimum(jnp.maximum(entries, -bound), bound).astype(held_as)


def setup_inputs(seed: int = 0) -> dict:
    key_list = jax.random.split(jax.random.key(seed), 11)
    return {
        "fields": draw_fields(jax.random.fold_in(key_list[10], 71), 0),
        "cotangent": gaussian(key_list[1], (MEMBERS, CHANNELS, LOCATION_NUMBER), 1.0, 6.0, ((0, 4), (2, 32))),
        "w_query": gaussian(key_list[2], (CHANNELS, CHANNELS), CHANNELS ** -0.5, 0.75),
        "w_key": gaussian(key_list[3], (CHANNELS, CHANNELS), CHANNELS ** -0.5, 0.75),
        "w_value": gaussian(key_list[4], (CHANNELS, CHANNELS), CHANNELS ** -0.5, 0.75),
        "w_out": gaussian(key_list[5], (CHANNELS, CHANNELS), CHANNELS ** -0.5, 0.75),
        "w_up": gaussian(key_list[6], (INNER, CHANNELS), CHANNELS ** -0.5, 0.75),
        "w_down": gaussian(key_list[7], (CHANNELS, INNER), INNER ** -0.5, 0.375),
        "gain_attn": jnp.clip(1.0 + 0.18 * jax.random.normal(key_list[8], (CHANNELS,), jnp.float32), 0.1, 1.9),
        "gain_mlp": jnp.clip(1.0 + 0.18 * jax.random.normal(key_list[9], (CHANNELS,), jnp.float32), 0.1, 1.9),
    }


norm_eps = 1e-05
lat_span = 1.4
sharpness_divisor = 32.0

def mul(form, left, right):
    return jnp.einsum(form, left.astype(jnp.float32), right.astype(jnp.float32))

def channel_norm(field, gain):
    values = field.astype(jnp.float32)
    center = values - lax.optimization_barrier(jnp.mean(values, axis=1, keepdims=True))
    spread = lax.rsqrt(lax.optimization_barrier(jnp.mean(center * center, axis=1, keepdims=True)) + norm_eps)
    normed = center * spread
    return ((normed * gain[None, :, None]).astype(jnp.bfloat16), normed, spread)

def norm_back(grad_normed, normed, spread, gain):
    scaled = grad_normed * gain[None, :, None]
    return spread * (scaled - lax.optimization_barrier(jnp.mean(scaled, axis=1, keepdims=True)) - normed * lax.optimization_barrier(jnp.mean(scaled * normed, axis=1, keepdims=True)))

def project(weight_matrix, field):
    return mul('oc,mcg->mog', weight_matrix, field)

def project_back(weight_matrix, grad):
    return mul('oc,mog->mcg', weight_matrix, grad)

def outer_sum(grad, field):
    return mul('mog,mcg->oc', grad, field)

def later_half(rows, mixed, grads_in, w_out, w_up, w_down, gain_mlp):
    resid = rows.astype(jnp.float32) + project(w_out, mixed)
    normed2, hat2, spread2 = channel_norm(resid, gain_mlp)
    inner = project(w_up, normed2)
    sig = jax.nn.sigmoid(inner)
    hidden = (inner * sig).astype(jnp.bfloat16)
    result = (resid + project(w_down, hidden)).astype(jnp.bfloat16)
    grad_inner = (project_back(w_down, grads_in) * sig * (1.0 + inner * (1.0 - sig))).astype(jnp.bfloat16)
    grad_normed2 = project_back(w_up, grad_inner)
    grad_resid = grads_in.astype(jnp.float32) + norm_back(grad_normed2, hat2, spread2, gain_mlp)
    grad_resid_b = grad_resid.astype(jnp.bfloat16)
    grad_mixed = project_back(w_out, grad_resid_b).astype(jnp.bfloat16)
    grads = (outer_sum(grad_resid_b, mixed), outer_sum(grad_inner, normed2), outer_sum(grads_in, hidden), lax.optimization_barrier(jnp.sum(grad_normed2 * hat2, axis=(0, 2))))
    return (result, grad_resid, grad_mixed, grads)

def reference(fields, cotangent, w_query, w_key, w_value, w_out, w_up, w_down, gain_attn, gain_mlp):
    position = (jnp.arange(LOCATION_NUMBER, dtype=jnp.int32) % G_DEV).astype(jnp.float32)
    lat_weight = jnp.cos(lat_span * (position + 0.5) / G_DEV)
    attention_divisor = sharpness_divisor / (FEATURE_PER_PART * LOCATION_NUMBER)

    def first(row):
        normed1, hat1, spread1 = channel_norm(row[None], gain_attn)
        query = (project(w_query, normed1) * lat_weight).astype(jnp.bfloat16)
        key = project(w_key, normed1).astype(jnp.bfloat16)
        value = project(w_value, normed1).astype(jnp.bfloat16)
        return (query[0], key[0], value[0])
    query, key, value = lax.map(first, fields)

    def to_heads(tensor):
        return tensor.reshape(MEMBERS, HEADS, FEATURE_PER_PART, LOCATION_NUMBER).transpose(1, 0, 2, 3)

    def from_heads(tensor):
        return tensor.transpose(1, 0, 2, 3).reshape(MEMBERS, CHANNELS, LOCATION_NUMBER)

    def attend(parts):
        qpart, kpart, vpart = parts
        scores = attention_divisor * mul('idg,jdg->ij', qpart, kpart)
        expo = jnp.exp(scores)
        probs = expo / lax.optimization_barrier(jnp.sum(expo, axis=1, keepdims=True))
        probs_b = probs.astype(jnp.bfloat16)
        mixed = mul('ij,jdg->idg', probs_b, vpart).astype(jnp.bfloat16)
        return (probs, probs_b, mixed)
    probs, probs_b, blended_parts = lax.map(attend, (to_heads(query), to_heads(key), to_heads(value)))
    mixed = from_heads(blended_parts)

    def second(parts):
        row, mix, grad_row = parts
        result, grad_resid, grad_mixed, grads = later_half(row[None], mix[None], grad_row[None], w_out, w_up, w_down, gain_mlp)
        return (result[0], grad_resid[0], grad_mixed[0], grads)
    result, grad_resid, grad_mixed, mlp_grads = lax.map(second, (fields, mixed, cotangent))
    grad_w_out, grad_w_up, grad_w_down, grad_gain_mlp = [lax.optimization_barrier(jnp.sum(t, axis=0)) for t in mlp_grads]

    def attend_back(parts):
        prob, prob_b, qpart, kpart, vpart, gpart = parts
        dots = mul('idg,jdg->ij', gpart, vpart)
        grad_scores = (attention_divisor * prob * (dots - lax.optimization_barrier(jnp.sum(prob * dots, axis=1, keepdims=True)))).astype(jnp.bfloat16)
        grad_value = mul('ij,idg->jdg', prob_b, gpart).astype(jnp.bfloat16)
        grad_query = mul('ij,jdg->idg', grad_scores, kpart)
        grad_key = mul('ij,idg->jdg', grad_scores, qpart).astype(jnp.bfloat16)
        return (grad_query, grad_key, grad_value)
    gq, gk, gv = lax.map(attend_back, (probs, probs_b, to_heads(query), to_heads(key), to_heads(value), to_heads(grad_mixed)))
    grad_query = (from_heads(gq) * lat_weight).astype(jnp.bfloat16)
    grad_key = from_heads(gk)
    grad_value = from_heads(gv)

    def third(parts):
        row, gqr, gkr, gvr, grr = parts
        normed1, hat1, spread1 = channel_norm(row[None], gain_attn)
        grad_normed1 = project_back(w_query, gqr[None]) + project_back(w_key, gkr[None]) + project_back(w_value, gvr[None])
        grad_row = (grr[None] + norm_back(grad_normed1, hat1, spread1, gain_attn)).astype(jnp.bfloat16)
        return (grad_row[0], outer_sum(gqr[None], normed1), outer_sum(gkr[None], normed1), outer_sum(gvr[None], normed1), lax.optimization_barrier(jnp.sum(grad_normed1 * hat1, axis=(0, 2))))
    grad_fields, gwq, gwk, gwv, gga = lax.map(third, (fields, grad_query, grad_key, grad_value, grad_resid))
    return (result, grad_fields, lax.optimization_barrier(jnp.sum(gwq, axis=0)), lax.optimization_barrier(jnp.sum(gwk, axis=0)), lax.optimization_barrier(jnp.sum(gwv, axis=0)), grad_w_out, grad_w_up, grad_w_down, lax.optimization_barrier(jnp.sum(gga, axis=0)), grad_gain_mlp)
```

```python
import functools

import jax
import jax.numpy as jnp
from jax import lax
from jax.experimental import pallas as pl
from jax.experimental.pallas import tpu as pltpu
from jax.sharding import PartitionSpec as P

HEADS = 4

norm_eps = 1e-05
lat_span = 1.4
sharpness_divisor = 32.0

VMEM_LIMIT = 56 * 1024 * 1024
f32 = jnp.float32
bf16 = jnp.bfloat16


def dot(left, right):
    return lax.dot_general(left, right, (((1,), (0,)), ((), ())), preferred_element_type=f32)


def dot_t(left, right):
    return lax.dot_general(left, right, (((1,), (1,)), ((), ())), preferred_element_type=f32)


def channel_hat(values):
    center = values - jnp.mean(values, axis=0, keepdims=True)
    spread = lax.rsqrt(jnp.mean(center * center, axis=0, keepdims=True) + norm_eps)
    return center * spread, spread


def norm_back(scaled, hat, spread):
    return spread * (
        scaled
        - jnp.mean(scaled, axis=0, keepdims=True)
        - hat * jnp.mean(scaled * hat, axis=0, keepdims=True)
    )


def member_rows(members, part):
    shape = (members * part, members)
    row = lax.broadcasted_iota(jnp.int32, shape, 0)
    column = lax.broadcasted_iota(jnp.int32, shape, 1)
    return row // part == column


def same_channel(members, part):
    shape = (members * part, members * part)
    row = lax.broadcasted_iota(jnp.int32, shape, 0)
    column = lax.broadcasted_iota(jnp.int32, shape, 1)
    return row % part == column % part


def head_rows(ref, head, part):
    members, _, cells = ref.shape
    return ref[:, head * part : (head + 1) * part, :].reshape(members * part, cells)


def pair_sums(left_ref, right_ref, out_ref):
    members, channels, _ = left_ref.shape
    part = channels // HEADS
    same = same_channel(members, part)
    collect = member_rows(members, part).astype(f32)
    sums = []
    for head in range(HEADS):
        pairs = dot_t(head_rows(left_ref, head, part), head_rows(right_ref, head, part))
        pairs = jnp.where(same, pairs, 0.0).reshape(members, part, members * part)
        lanes = jnp.sum(pairs, axis=1)
        sums.append(
            lax.dot_general(
                lanes,
                collect,
                (((1,), (0,)), ((), ())),
                precision=lax.Precision.HIGHEST,
                preferred_element_type=f32,
            )
        )
    out_ref[...] = jnp.concatenate(sums, axis=1)


def softmax_probs(score_sums, head, divisor):
    members = score_sums.shape[0]
    expo = jnp.exp(score_sums[:, head * members : (head + 1) * members] * divisor)
    return expo / jnp.sum(expo, axis=1, keepdims=True)


def per_channel(weights, spread, same, transposed):
    rows = (dot_t if transposed else dot)(spread, weights).astype(bf16)
    return jnp.where(same, dot_t(rows, spread), 0.0).astype(bf16)


def first_kernel(
    place, x0, x1, x2, x3, w_qkv, gain, lat, rows_out, q_out, k_out, v_out, sums_out, q_all, k_all
):
    step = pl.program_id(0)
    block, channels, _ = x0.shape
    base = (place[0] ^ step) * block

    def work(x_ref):
        def member(i, carry):
            raw = x_ref[i]
            hat, _ = channel_hat(raw.astype(f32))
            normed = (hat * gain[...]).astype(bf16)
            qkv = dot(w_qkv[...], normed)
            query = (qkv[:channels] * lat[...]).astype(bf16)
            key = qkv[channels : 2 * channels].astype(bf16)
            rows_out[i] = raw
            q_out[i] = query
            k_out[i] = key
            v_out[i] = qkv[2 * channels :].astype(bf16)
            q_all[base + i] = query
            k_all[base + i] = key
            return carry

        lax.fori_loop(0, block, member, 0, unroll=2)

    for d, x_ref in enumerate((x0, x1, x2, x3)):
        pl.when(step == d)(functools.partial(work, x_ref))

    @pl.when(step == pl.num_programs(0) - 1)
    def _():
        pair_sums(q_all, k_all, sums_out)


def middle_kernel(
    divisor,
    sums,
    v_all,
    rows,
    cot,
    w_out,
    w_out_t,
    w_up,
    w_up_t,
    w_down,
    w_down_t,
    gain,
    result_out,
    resid_out,
    mixed_grad_out,
    dots_out,
    g_up_out,
    g_down_out,
    g_out_out,
    g_gain_out,
    mixed_all,
    grad_all,
):
    step = pl.program_id(0)
    block, channels, cells = rows.shape
    members = v_all.shape[0]
    part = channels // HEADS

    @pl.when(step == 0)
    def _():
        spread = member_rows(members, part).astype(bf16)
        same = same_channel(members, part)
        score_sums = sums[...]
        for head in range(HEADS):
            probs = softmax_probs(score_sums, head, divisor).astype(bf16)
            matrix = per_channel(probs, spread, same, False)
            mixed = dot(matrix, head_rows(v_all, head, part)).astype(bf16)
            mixed_all[:, head * part : (head + 1) * part, :] = mixed.reshape(members, part, cells)
        g_up_out[...] = jnp.zeros_like(g_up_out)
        g_down_out[...] = jnp.zeros_like(g_down_out)
        g_out_out[...] = jnp.zeros_like(g_out_out)
        g_gain_out[...] = jnp.zeros_like(g_gain_out)

    base = step * block

    def member(i, carry):
        mixed = mixed_all[base + i]
        grads_in = cot[i]
        resid = rows[i].astype(f32) + dot(w_out[...], mixed)
        hat, spread = channel_hat(resid)
        normed = (hat * gain[...]).astype(bf16)
        inner = dot(w_up[...], normed)
        sig = 0.5 * jnp.tanh(0.5 * inner) + 0.5
        hidden = (inner * sig).astype(bf16)
        result_out[i] = (resid + dot(w_down[...], hidden)).astype(bf16)
        grad_inner = (
            dot(w_down_t[...], grads_in) * (sig * (1.0 + inner * (1.0 - sig)))
        ).astype(bf16)
        grad_normed = dot(w_up_t[...], grad_inner)
        grad_resid = grads_in.astype(f32) + norm_back(grad_normed * gain[...], hat, spread)
        resid_out[i] = grad_resid
        grad_resid_b = grad_resid.astype(bf16)
        grad_mixed = dot(w_out_t[...], grad_resid_b).astype(bf16)
        mixed_grad_out[i] = grad_mixed
        grad_all[base + i] = grad_mixed
        g_up_out[...] += dot_t(grad_inner, normed)
        g_down_out[...] += dot_t(hidden, grads_in)
        g_out_out[...] += dot_t(grad_resid_b, mixed)
        g_gain_out[...] += jnp.sum(grad_normed * hat, axis=1, keepdims=True)
        return carry

    lax.fori_loop(0, block, member, 0, unroll=2)

    @pl.when(step == pl.num_programs(0) - 1)
    def _():
        pair_sums(grad_all, v_all, dots_out)


def last_kernel(
    divisor,
    sums,
    dots,
    q_all,
    k_all,
    grad_all,
    rows,
    resid,
    w_qkv_t,
    gain,
    lat,
    rows_out,
    g_qkv_out,
    g_gain_out,
    qkv_all,
):
    step = pl.program_id(0)
    block, channels, cells = rows.shape
    members = q_all.shape[0]
    part = channels // HEADS

    @pl.when(step == 0)
    def _():
        spread = member_rows(members, part).astype(bf16)
        same = same_channel(members, part)
        score_sums = sums[...]
        dot_sums = dots[...]
        for head in range(HEADS):
            probs = softmax_probs(score_sums, head, divisor)
            own = dot_sums[:, head * members : (head + 1) * members]
            grad_scores = (
                divisor * probs * (own - jnp.sum(probs * own, axis=1, keepdims=True))
            ).astype(bf16)
            probs = probs.astype(bf16)

            def place(offset, value, head=head):
                start = offset + head * part
                qkv_all[:, start : start + part, :] = value.astype(bf16).reshape(
                    members, part, cells
                )

            matrix = per_channel(grad_scores, spread, same, False)
            place(0, dot(matrix, head_rows(k_all, head, part)) * lat[...])
            matrix = per_channel(grad_scores, spread, same, True)
            place(channels, dot(matrix, head_rows(q_all, head, part)))
            matrix = per_channel(probs, spread, same, True)
            place(2 * channels, dot(matrix, head_rows(grad_all, head, part)))
        g_qkv_out[...] = jnp.zeros_like(g_qkv_out)
        g_gain_out[...] = jnp.zeros_like(g_gain_out)

    base = step * block

    def member(i, carry):
        hat, spread = channel_hat(rows[i].astype(f32))
        normed = (hat * gain[...]).astype(bf16)
        qkv = qkv_all[base + i]
        grad_normed = dot(w_qkv_t[...], qkv)
        rows_out[i] = (resid[i] + norm_back(grad_normed * gain[...], hat, spread)).astype(bf16)
        g_qkv_out[...] += dot_t(qkv, normed)
        g_gain_out[...] += jnp.sum(grad_normed * hat, axis=1, keepdims=True)
        return carry

    lax.fori_loop(0, block, member, 0, unroll=2)


def params():
    return pltpu.CompilerParams(
        vmem_limit_bytes=VMEM_LIMIT, dimension_semantics=("arbitrary",)
    )


def whole(array):
    return pl.BlockSpec(array.shape, lambda step, *_: (0,) * array.ndim)


def shape(dims, dtype):
    return jax.ShapeDtypeStruct(dims, dtype)


def first_call(place, blocks, w_qkv, gain, lat):
    block, channels, cells = blocks[0].shape
    groups = len(blocks)
    members = block * groups
    field = shape((members, channels, cells), bf16)
    spec = pl.BlockSpec((block, channels, cells), lambda d, place: (place[0] ^ d, 0, 0))
    sums = shape((members, HEADS * members), f32)
    operands = (*blocks, w_qkv, gain, lat)
    return pl.pallas_call(
        first_kernel,
        grid_spec=pltpu.PrefetchScalarGridSpec(
            num_scalar_prefetch=1,
            grid=(groups,),
            in_specs=[whole(t) for t in operands],
            out_specs=[spec] * 4 + [whole(sums)],
            scratch_shapes=[pltpu.VMEM(field.shape, bf16)] * 2,
        ),
        out_shape=[field] * 4 + [sums],
        compiler_params=params(),
    )(place, *operands)


def middle_call(divisor, block, sums, v_all, rows, cot, weights, gain):
    members, channels, cells = rows.shape
    w_out, w_up, w_down = weights
    inner = w_up.shape[0]
    spec = pl.BlockSpec((block, channels, cells), lambda step: (step, 0, 0))
    outs = [
        shape((members, channels, cells), bf16),
        shape((members, channels, cells), f32),
        shape((members, channels, cells), bf16),
        shape(sums.shape, f32),
        shape((inner, channels), f32),
        shape((inner, channels), f32),
        shape((channels, channels), f32),
        shape((channels, 1), f32),
    ]
    constants = (w_out, w_out.T, w_up, w_up.T, w_down, w_down.T, gain)
    return pl.pallas_call(
        functools.partial(middle_kernel, divisor),
        grid=(members // block,),
        in_specs=[whole(sums), whole(v_all), spec, spec] + [whole(t) for t in constants],
        out_specs=[spec] * 3 + [whole(t) for t in outs[3:]],
        scratch_shapes=[pltpu.VMEM((members, channels, cells), bf16)] * 2,
        out_shape=outs,
        compiler_params=params(),
    )(sums, v_all, rows, cot, *constants)


def last_call(divisor, block, sums, dots, q_all, k_all, grad_all, rows, resid, w_qkv, gain, lat):
    members, channels, cells = rows.shape
    spec = pl.BlockSpec((block, channels, cells), lambda step: (step, 0, 0))
    outs = [
        shape((members, channels, cells), bf16),
        shape(w_qkv.shape, f32),
        shape((channels, 1), f32),
    ]
    front = (sums, dots, q_all, k_all, grad_all)
    constants = (w_qkv.T, gain, lat)
    return pl.pallas_call(
        functools.partial(last_kernel, divisor),
        grid=(members // block,),
        in_specs=[whole(t) for t in front] + [spec, spec] + [whole(t) for t in constants],
        out_specs=[spec] + [whole(t) for t in outs[1:]],
        scratch_shapes=[pltpu.VMEM((members, 3 * channels, cells), bf16)],
        out_shape=outs,
        compiler_params=params(),
    )(*front, rows, resid, *constants)


def exchange(array, distance, axis="member"):
    size = lax.axis_size(axis)
    return lax.ppermute(array, axis, [(i, i ^ distance) for i in range(size)])


def member_sum(array):
    size = lax.axis_size("member")
    distance = 1
    while distance < size:
        array = array + exchange(array, distance)
        distance *= 2
    return array


def gather_sum(array):
    array = member_sum(array)
    size = lax.axis_size("grid")
    copies = jnp.broadcast_to(array[None], (size,) + array.shape)
    return jnp.sum(lax.all_to_all(copies, "grid", 0, 0), axis=0)


def scatter_sum(array):
    array = member_sum(array)
    size = lax.axis_size("grid")
    pieces = array.reshape(size, array.shape[0] // size, array.shape[1])
    own = jnp.sum(lax.all_to_all(pieces, "grid", 0, 0), axis=0)
    copies = jnp.broadcast_to(own[None], (size,) + own.shape)
    return lax.all_to_all(copies, "grid", 0, 0).reshape(array.shape)


def shards(fields, cotangent, w_query, w_key, w_value, w_out, w_up, w_down, gain_attn, gain_mlp):
    block, channels, tile = fields.shape
    groups = lax.axis_size("member")
    me = lax.axis_index("member")
    width = tile // groups
    divisor = sharpness_divisor / ((channels // HEADS) * tile * lax.axis_size("grid"))

    def outgoing(array, d):
        return lax.dynamic_slice_in_dim(array, (me ^ d) * width, width, axis=2)

    def incoming(array):
        return [outgoing(array, 0)] + [exchange(outgoing(array, d), d) for d in range(1, groups)]

    def outward(array):
        whole_tile = jnp.zeros((block, channels, tile), array.dtype)
        for d in range(groups):
            piece = lax.dynamic_slice_in_dim(array, (me ^ d) * block, block, axis=0)
            if d:
                piece = exchange(piece, d)
            whole_tile = lax.dynamic_update_slice_in_dim(whole_tile, piece, (me ^ d) * width, 2)
        return whole_tile

    position = (me * width).astype(f32) + jnp.arange(width, dtype=f32)
    lat = jnp.cos(lat_span * (position + 0.5) / tile)[None, :]
    w_qkv = jnp.concatenate([w_query, w_key, w_value], axis=0)
    gain_a, gain_m = gain_attn[:, None], gain_mlp[:, None]

    rows, q_all, k_all, v_all, sums = first_call(
        me[None].astype(jnp.int32), incoming(fields), w_qkv, gain_a, lat
    )
    pieces = incoming(cotangent)
    cot = jnp.zeros((block * groups, channels, width), bf16)
    for d, piece in enumerate(pieces):
        cot = lax.dynamic_update_slice_in_dim(cot, piece, (me ^ d) * block, 0)
    sums = gather_sum(sums)

    result, resid, grad_all, dots, g_up, g_down_t, g_out, g_gain_m = middle_call(
        divisor, block // 2, sums, v_all, rows, cot, (w_out, w_up, w_down), gain_m
    )
    result = outward(result)
    dots = gather_sum(dots)

    grad_rows, g_qkv, g_gain_a = last_call(
        divisor, block // 2, sums, dots, q_all, k_all, grad_all, rows, resid, w_qkv, gain_a, lat
    )
    grad_fields = outward(grad_rows)

    gains = jnp.pad(jnp.concatenate([g_gain_a, g_gain_m], axis=1), ((0, 0), (0, channels - 2)))
    left = jnp.concatenate([g_up, g_qkv], axis=0)
    right = jnp.concatenate([g_down_t, g_out, gains, jnp.zeros((channels, channels), f32)], axis=0)
    total = scatter_sum(jnp.concatenate([left, right], axis=1))
    inner = w_up.shape[0]
    left, right = total[:, :channels], total[:, channels:]
    g_up, g_qkv = left[:inner], left[inner:]
    g_down, g_out = right[:inner].T, right[inner : inner + channels]
    gains = right[inner + channels : inner + 2 * channels]
    return (
        result,
        grad_fields,
        g_qkv[:channels],
        g_qkv[channels : 2 * channels],
        g_qkv[2 * channels :],
        g_out,
        g_up,
        g_down,
        gains[:, 0],
        gains[:, 1],
    )


def solution(mesh):
    split = P("member", None, "grid")
    return jax.shard_map(
        shards,
        mesh=mesh,
        in_specs=(split, split) + (P(),) * 8,
        out_specs=(split, split) + (P(),) * 8,
        check_vma=False,
    )
```

```python
import functools

import jax
import jax.numpy as jnp
from jax import lax
from jax.experimental import pallas as pl
from jax.experimental.pallas import tpu as pltpu
from jax.sharding import PartitionSpec as P

HEADS = 4

norm_eps = 1e-05
lat_span = 1.4
sharpness_divisor = 32.0

VMEM_LIMIT = 40 * 1024 * 1024
UNROLL = 4
Z_PARTS = 2
f32 = jnp.float32
bf16 = jnp.bfloat16


def dot(left, right):
    return lax.dot_general(left, right, (((1,), (0,)), ((), ())), preferred_element_type=f32)


def dot_t(left, right):
    return lax.dot_general(left, right, (((1,), (1,)), ((), ())), preferred_element_type=f32)


def channel_hat(values):
    center = values - jnp.mean(values, axis=0, keepdims=True)
    spread = lax.rsqrt(jnp.mean(center * center, axis=0, keepdims=True) + norm_eps)
    return center * spread, spread


def norm_back(scaled, hat, spread):
    return spread * (
        scaled
        - jnp.mean(scaled, axis=0, keepdims=True)
        - hat * jnp.mean(scaled * hat, axis=0, keepdims=True)
    )


def member_rows(members, part):
    shape = (members * part, members)
    row = lax.broadcasted_iota(jnp.int32, shape, 0)
    column = lax.broadcasted_iota(jnp.int32, shape, 1)
    return lax.div(row, part) == column


def same_channel(members, part):
    shape = (members * part, members * part)
    row = lax.broadcasted_iota(jnp.int32, shape, 0)
    column = lax.broadcasted_iota(jnp.int32, shape, 1)
    return lax.rem(row, part) == lax.rem(column, part)


def head_rows(ref, head, part):
    members, _, cells = ref.shape
    return ref[:, head * part : (head + 1) * part, :].reshape(members * part, cells)


def pair_sums(left_ref, right_ref, out_ref):
    members, channels, _ = left_ref.shape
    part = channels // HEADS
    same = same_channel(members, part)
    collect = member_rows(members, part).astype(f32)
    sums = []
    for head in range(HEADS):
        pairs = dot_t(head_rows(left_ref, head, part), head_rows(right_ref, head, part))
        pairs = jnp.where(same, pairs, 0.0).reshape(members, part, members * part)
        lanes = jnp.sum(pairs, axis=1)
        sums.append(
            lax.dot_general(
                lanes,
                collect,
                (((1,), (0,)), ((), ())),
                precision=lax.Precision.HIGHEST,
                preferred_element_type=f32,
            )
        )
    out_ref[...] = jnp.concatenate(sums, axis=1)


def softmax_probs(score_sums, head, divisor):
    members = score_sums.shape[0]
    expo = jnp.exp(score_sums[:, head * members : (head + 1) * members] * divisor)
    return expo / jnp.sum(expo, axis=1, keepdims=True)


def per_channel(weights, spread, same, transposed):
    rows = (dot_t if transposed else dot)(spread, weights).astype(bf16)
    return jnp.where(same, dot_t(rows, spread), 0.0).astype(bf16)


def loop(count, body):
    def step(i, carry):
        body(i)
        return carry

    lax.fori_loop(0, count, step, 0, unroll=UNROLL)


def start(copies):
    for copy in copies:
        copy.start()
    return copies


def wait(copies):
    for copy in copies:
        copy.wait()


def own_cells(place, ref, width):
    return ref.at[:, :, pl.ds(pl.multiple_of(place[0] * width, width), width)]


def first_kernel(
    place, fields, x1, x2, x3, w_qkv, gain, lat, q_out, k_out, v_out, sums, x, q_all, k_all, v_all, sin, sout
):
    groups, block, channels, cells = x.shape
    sources = (own_cells(place, fields, cells), x1, x2, x3)
    arrive = start(
        [pltpu.make_async_copy(t, x.at[d], sin.at[d]) for d, t in enumerate(sources)]
    )
    leave = []
    for d in range(groups):
        base = (place[0] ^ d) * block
        arrive[d].wait()

        def member(i, base=base, d=d):
            hat, _ = channel_hat(x[d, i].astype(f32))
            normed = (hat * gain[...]).astype(bf16)
            qkv = dot(w_qkv[...], normed)
            q_all[base + i] = (qkv[:channels] * lat[...]).astype(bf16)
            k_all[base + i] = qkv[channels : 2 * channels].astype(bf16)
            v_all[base + i] = qkv[2 * channels :].astype(bf16)

        loop(block, member)
        for n, (here, there) in enumerate(((q_all, q_out), (k_all, k_out), (v_all, v_out))):
            at = pl.ds(base, block)
            leave += start([pltpu.make_async_copy(here.at[at], there.at[at], sout.at[n, d])])
    pair_sums(q_all, k_all, sums)
    wait(leave)


def later_half(mixed, raw, grads_in, weights, result, resid_out, mixed_grad, grads):
    w_out, w_out_t, w_up, w_up_t, w_down, w_down_t, gain = weights
    g_up, g_down, g_out, g_gain = grads
    resid = raw.astype(f32) + dot(w_out[...], mixed)
    hat, spread = channel_hat(resid)
    normed = (hat * gain[...]).astype(bf16)
    inner = dot(w_up[...], normed)
    sig = 0.5 * jnp.tanh(0.5 * inner) + 0.5
    hidden = (inner * sig).astype(bf16)
    result[...] = (resid + dot(w_down[...], hidden)).astype(bf16)
    grad_inner = (
        dot(w_down_t[...], grads_in) * (sig * (1.0 + inner * (1.0 - sig)))
    ).astype(bf16)
    grad_normed = dot(w_up_t[...], grad_inner)
    grad_resid = grads_in.astype(f32) + norm_back(grad_normed * gain[...], hat, spread)
    resid_out[...] = grad_resid
    grad_resid_b = grad_resid.astype(bf16)
    mixed_grad[...] = dot(w_out_t[...], grad_resid_b).astype(bf16)
    g_up[...] += dot_t(grad_inner, normed)
    g_down[...] += dot_t(hidden, grads_in)
    g_out[...] += dot_t(grad_resid_b, mixed)
    g_gain[...] += jnp.sum(grad_normed * hat, axis=1, keepdims=True)


def far_kernel(divisor, *refs):
    place, sums, more_sums, v_hbm, x2, x3, c2, c3 = refs[:8]
    weights, refs = refs[8:15], refs[15:]
    outs, near_out, grads, refs = refs[:4], refs[4], refs[5:9], refs[9:]
    v_all, mixed_all, x, c, result, resid, grad, sin, sout = refs
    members, channels, cells = v_all.shape
    block = members // 4
    part = channels // HEADS
    arrive = start(
        [
            pltpu.make_async_copy(here, there, sin.at[n])
            for n, (here, there) in enumerate(
                ((v_hbm, v_all), (x2, x.at[0]), (c2, c.at[0]), (x3, x.at[1]), (c3, c.at[1]))
            )
        ]
    )
    for ref in grads:
        ref[...] = jnp.zeros_like(ref)
    spread = member_rows(members, part).astype(bf16)
    same = same_channel(members, part)
    score_sums = sums[...] + more_sums[...]
    arrive[0].wait()
    for head in range(HEADS):
        probs = softmax_probs(score_sums, head, divisor).astype(bf16)
        matrix = per_channel(probs, spread, same, False)
        mixed = dot(matrix, head_rows(v_all, head, part)).astype(bf16)
        mixed_all[:, head * part : (head + 1) * part, :] = mixed.reshape(members, part, cells)
    leave = start(
        [
            pltpu.make_async_copy(
                mixed_all.at[pl.ds((place[0] ^ d) * block, block)], near_out.at[d], sout.at[d]
            )
            for d in range(2)
        ]
    )
    for n in range(2):
        base = (place[0] ^ (2 + n)) * block
        wait(arrive[1 + 2 * n : 3 + 2 * n])

        def member(i, base=base, n=n):
            later_half(
                mixed_all[base + i],
                x[n, i],
                c[n, i],
                weights,
                result.at[n, i],
                resid.at[n, i],
                grad.at[n, i],
                grads,
            )

        loop(block, member)
        leave += start(
            [
                pltpu.make_async_copy(result.at[n], outs[n], sout.at[2 + n]),
                pltpu.make_async_copy(resid.at[n], outs[2].at[n], sout.at[4 + n]),
                pltpu.make_async_copy(grad.at[n], outs[3].at[n], sout.at[6 + n]),
            ]
        )
    wait(leave)


def near_kernel(*refs):
    place, v_hbm, fields, x1, cotangent, c1, near, far_grad = refs[:8]
    weights, begun, refs = refs[8:15], refs[15:19], refs[19:]
    outs, (own, other), refs = refs[:4], refs[4:6], refs[6:]
    v_all, grad_all, mixed, x, c, result, resid, g_up, g_down, g_out, g_gain, early, sin, sout = refs
    grads = (g_up, g_down, g_out, g_gain)
    members, channels, cells = v_all.shape
    block = members // 4
    arrive = start(
        [
            pltpu.make_async_copy(here, there, sin.at[n])
            for n, (here, there) in enumerate(
                (
                    (near, mixed),
                    (own_cells(place, fields, cells), x.at[0]),
                    (own_cells(place, cotangent, cells), c.at[0]),
                    (x1, x.at[1]),
                    (c1, c.at[1]),
                    (v_hbm, v_all),
                    (far_grad.at[0], grad_all.at[pl.ds((place[0] ^ 2) * block, block)]),
                    (far_grad.at[1], grad_all.at[pl.ds((place[0] ^ 3) * block, block)]),
                )
            )
        ]
    )
    for ref, value in zip(grads, begun):
        ref[...] = value[...]
    arrive[0].wait()
    leave = []
    for n in range(2):
        base = (place[0] ^ n) * block
        wait(arrive[1 + 2 * n : 3 + 2 * n])

        def member(i, base=base, n=n):
            later_half(
                mixed[n, i],
                x[n, i],
                c[n, i],
                weights,
                result.at[n, i],
                resid.at[n, i],
                grad_all.at[base + i],
                grads,
            )

        loop(block, member)
        leave += start(
            [
                pltpu.make_async_copy(result.at[n], outs[n], sout.at[n]),
                pltpu.make_async_copy(resid.at[n], outs[2].at[n], sout.at[2 + n]),
                pltpu.make_async_copy(
                    grad_all.at[pl.ds(base, block)], outs[3].at[n], sout.at[4 + n]
                ),
            ]
        )
    wait(arrive[5:])
    pair_sums(grad_all, v_all, own.at[:members])
    inner = g_up.shape[0]
    early[:inner, :channels] = g_up[...]
    early[:inner, channels:] = g_down[...]
    early[inner:, :channels] = g_out[...]
    early[inner:, channels:] = jnp.broadcast_to(g_gain[...], g_out.shape)
    half = early.shape[0] // 2
    core = lax.rem(place[0], 2)
    other[:members] = own[:members]
    own[members:] = early[pl.ds(pl.multiple_of(core * half, 8), half), :]
    other[members:] = early[pl.ds(pl.multiple_of((1 - core) * half, 8), half), :]
    wait(leave)


def last_kernel(divisor, *refs):
    place, sums, more_sums, dots, more_dots, q_hbm, k_hbm, near_grad, far_grad = refs[:9]
    fields, x1, x2, x3, near_resid, far_resid, w_qkv_t, gain, lat = refs[9:18]
    rows_out, own, other, refs = refs[18:22], refs[22], refs[23], refs[24:]
    q_all, k_all, grad_all, x, resid, rows, qkv_all, g_qkv, g_gain, late, sin, sout = refs
    members, channels, cells = q_all.shape
    part = channels // HEADS
    block = members // 4
    moves = [(k_hbm, k_all), (q_hbm, q_all)]
    for d in range(4):
        source = (near_grad if d < 2 else far_grad).at[d % 2]
        moves.append((source, grad_all.at[pl.ds((place[0] ^ d) * block, block)]))
    for d, source in ((2, x2), (3, x3), (1, x1), (0, own_cells(place, fields, cells))):
        moves.append((source, x.at[d]))
        moves.append(((near_resid if d < 2 else far_resid).at[d % 2], resid.at[d]))
    arrive = start(
        [pltpu.make_async_copy(here, there, sin.at[n]) for n, (here, there) in enumerate(moves)]
    )
    g_qkv[...] = jnp.zeros_like(g_qkv)
    g_gain[...] = jnp.zeros_like(g_gain)
    spread = member_rows(members, part).astype(bf16)
    same = same_channel(members, part)
    score_sums = sums[...] + more_sums[...]
    dot_sums = dots[:members] + more_dots[:members]
    probs, grad_scores = [], []
    for head in range(HEADS):
        prob = softmax_probs(score_sums, head, divisor)
        one = dot_sums[:, head * members : (head + 1) * members]
        grad_scores.append(
            (divisor * prob * (one - jnp.sum(prob * one, axis=1, keepdims=True))).astype(bf16)
        )
        probs.append(prob.astype(bf16))

    def put(offset, head, value):
        begin = offset + head * part
        qkv_all[:, begin : begin + part, :] = value.astype(bf16).reshape(members, part, cells)

    arrive[0].wait()
    for head in range(HEADS):
        matrix = per_channel(grad_scores[head], spread, same, False)
        put(0, head, dot(matrix, head_rows(k_all, head, part)) * lat[...])
    arrive[1].wait()
    for head in range(HEADS):
        matrix = per_channel(grad_scores[head], spread, same, True)
        put(channels, head, dot(matrix, head_rows(q_all, head, part)))
    wait(arrive[2:6])
    for head in range(HEADS):
        matrix = per_channel(probs[head], spread, same, True)
        put(2 * channels, head, dot(matrix, head_rows(grad_all, head, part)))

    leave = []
    for n, d in enumerate((2, 3, 1, 0)):
        base = (place[0] ^ d) * block
        wait(arrive[6 + 2 * n : 8 + 2 * n])

        def member(i, base=base, d=d):
            hat, spread = channel_hat(x[d, i].astype(f32))
            normed = (hat * gain[...]).astype(bf16)
            qkv = qkv_all[base + i]
            grad_normed = dot(w_qkv_t[...], qkv)
            rows[d, i] = (resid[d, i] + norm_back(grad_normed * gain[...], hat, spread)).astype(bf16)
            g_qkv[...] += dot_t(qkv, normed)
            g_gain[...] += jnp.sum(grad_normed * hat, axis=1, keepdims=True)

        loop(block, member)
        leave += start([pltpu.make_async_copy(rows.at[d], rows_out[d], sout.at[d])])
    late[:channels, :channels] = g_qkv[:channels]
    late[:channels, channels:] = g_qkv[channels : 2 * channels]
    late[channels:, :channels] = g_qkv[2 * channels :]
    late[channels:, channels:] = jnp.broadcast_to(g_gain[...], (channels, channels))
    core = lax.rem(place[0], 2)
    own[...] = late[pl.ds(pl.multiple_of(core * channels, 8), channels), :]
    other[...] = late[pl.ds(pl.multiple_of((1 - core) * channels, 8), channels), :]
    wait(leave)


def call(kernel, operands, outs, scratch, arrive, leave, microseconds):
    def spec(inside):
        return pl.BlockSpec(memory_space=pltpu.VMEM if inside else pltpu.HBM)

    place, *operands = operands
    return pl.pallas_call(
        kernel,
        in_specs=[pl.BlockSpec(memory_space=pltpu.SMEM)] + [spec(t[1]) for t in operands],
        out_specs=[spec(t[1]) for t in outs],
        out_shape=[jax.ShapeDtypeStruct(*t) if near else pltpu.HBM(*t) for t, near in outs],
        scratch_shapes=[pltpu.VMEM(*t) for t in scratch]
        + [pltpu.SemaphoreType.DMA(arrive), pltpu.SemaphoreType.DMA(leave)],
        compiler_params=pltpu.CompilerParams(vmem_limit_bytes=VMEM_LIMIT),
        cost_estimate=pl.CostEstimate(
            flops=0, bytes_accessed=microseconds * 3_600_000, transcendentals=0
        ),
    )(
        place,
        *[
            t if near else pltpu.with_memory_space_constraint(t, pltpu.HBM) for t, near in operands
        ],
    )


def inside(*arrays):
    return [(t, True) for t in arrays]


def outside(*arrays):
    return [(t, False) for t in arrays]


def first_call(place, fields, received, w_qkv, gain, lat):
    block, channels, cells = received[0].shape
    members = block * 4
    field = ((members, channels, cells), bf16)
    sums = ((members, HEADS * members), f32)
    return call(
        first_kernel,
        [place] + outside(fields, *received) + inside(w_qkv, gain, lat),
        outside(field, field, field) + inside(sums),
        [((4, block, channels, cells), bf16), field, field, field],
        (4,),
        (3, 4),
        7,
    )


def far_call(divisor, place, sums, v_all, received, cots, constants):
    members, channels, cells = v_all.shape
    block = members // 4
    inner = constants[2].shape[0]
    field = ((members, channels, cells), bf16)
    one = ((block, channels, cells), bf16)
    pair = ((2, block, channels, cells), bf16)
    wide = (pair[0], f32)
    grads = [((inner, channels), f32)] * 2 + [((channels, channels), f32), ((channels, 1), f32)]
    return call(
        functools.partial(far_kernel, divisor),
        [place] + inside(*sums) + outside(v_all, *received, *cots) + inside(*constants),
        outside(one, one, wide, pair, pair) + inside(*grads),
        [field, field, pair, pair, pair, wide, pair],
        (5,),
        (8,),
        20,
    )


def near_call(place, v_all, fields, x1, cotangent, c1, near, far_grad, constants, grads):
    members, channels, cells = v_all.shape
    block = members // 4
    field = ((members, channels, cells), bf16)
    one = ((block, channels, cells), bf16)
    pair = ((2, block, channels, cells), bf16)
    wide = (pair[0], f32)
    early = grads[0].shape[0] + channels
    packed = ((members + early // 2, 2 * channels), f32)
    return call(
        near_kernel,
        [place]
        + outside(v_all, fields, x1, cotangent, c1, near, far_grad)
        + inside(*constants, *grads),
        outside(one, one, wide, pair) + inside(packed, packed),
        [field, field, pair, pair, pair, pair, wide]
        + [(t.shape, f32) for t in grads]
        + [((early, 2 * channels), f32)],
        (8,),
        (6,),
        20,
    )


def last_call(divisor, place, sums, dots, arrays, constants):
    q_all = arrays[0]
    members, channels, cells = q_all.shape
    block = members // 4
    field = ((members, channels, cells), bf16)
    one = ((block, channels, cells), bf16)
    four = ((4, block, channels, cells), bf16)
    half = ((channels, 2 * channels), f32)
    return call(
        functools.partial(last_kernel, divisor),
        [place] + inside(*sums, *dots) + outside(*arrays) + inside(*constants),
        outside(one, one, one, one) + inside(half, half),
        [field, field, field, four, (four[0], f32), four]
        + [((members, 3 * channels, cells), bf16), ((3 * channels, channels), f32)]
        + [((channels, 1), f32), ((2 * channels, 2 * channels), f32)],
        (14,),
        (4,),
        12,
    )


def exchange(array, distance, axis="member"):
    size = lax.axis_size(axis)
    return lax.ppermute(array, axis, [(i, i ^ distance) for i in range(size)])


def plane_groups():
    size = lax.axis_size("grid")
    return [list(range(part, size, Z_PARTS)) for part in range(Z_PARTS)]


def over_plane(pieces):
    return lax.all_to_all(pieces, "grid", 0, 0, axis_index_groups=plane_groups())


def copies(array):
    return jnp.broadcast_to(array[None], (lax.axis_size("grid") // Z_PARTS,) + array.shape)


def over_z(array):
    array = array + exchange(array, 2)
    return array, exchange(array, 1, "grid")


def together(*arrays):
    return lax.optimization_barrier(arrays)


def shards(fields, cotangent, w_query, w_key, w_value, w_out, w_up, w_down, gain_attn, gain_mlp):
    block, channels, tile = fields.shape
    groups = lax.axis_size("member")
    me = lax.axis_index("member")
    width = tile // groups
    members = block * groups
    inner = w_up.shape[0]
    divisor = sharpness_divisor / ((channels // HEADS) * tile * lax.axis_size("grid"))

    def outgoing(array):
        return [
            lax.dynamic_slice_in_dim(array, (me ^ d) * width, width, axis=2) for d in range(1, groups)
        ]

    def send(pieces, distances):
        return [exchange(piece, d) for piece, d in zip(pieces, distances)]

    def joined(pieces):
        whole_tile = jnp.zeros((block, channels, tile), bf16)
        for d, piece in enumerate(pieces):
            whole_tile = lax.dynamic_update_slice_in_dim(whole_tile, piece, (me ^ d) * width, 2)
        return whole_tile

    position = (me * width).astype(f32) + jnp.arange(width, dtype=f32)
    lat = jnp.cos(lat_span * (position + 0.5) / tile)[None, :]
    w_qkv = jnp.concatenate([w_query, w_key, w_value], axis=0)
    gain_a, gain_m = gain_attn[:, None], gain_mlp[:, None]
    place = me[None].astype(jnp.int32)
    constants = (w_out, w_out.T, w_up, w_up.T, w_down, w_down.T, gain_m)

    far = send(outgoing(fields)[1:], (2, 3))
    x1 = exchange(outgoing(fields)[0], 1)
    cots = outgoing(cotangent)
    far, x1, cots, w_qkv, gain_a, lat = together(far, x1, cots, w_qkv, gain_a, lat)
    received = [x1, *far]
    q_all, k_all, v_all, sums = first_call(place, fields, received, w_qkv, gain_a, lat)
    cots = send(cots, (1, 2, 3))

    sums = jnp.sum(over_plane(copies(sums + exchange(sums, 1))), axis=0)
    sums, cots = together(sums, cots)
    sums = over_z(sums)

    result2, result3, far_resid, far_grad, near, *begun = far_call(
        divisor, place, sums, v_all, received[1:], cots[1:], constants
    )
    result2, result3 = send((result2, result3), (2, 3))
    result0, result1, near_resid, near_grad, own, other = near_call(
        place, v_all, fields, x1, cotangent, cots[0], near, far_grad, constants, begun
    )
    own, other, result2, result3 = together(own, other, result2, result3)
    size = lax.axis_size("grid") // Z_PARTS
    own = own + exchange(other, 1)
    shares = own[members:].reshape(size, -1, own.shape[1])
    pieces = jnp.concatenate([copies(own[:members]), shares], axis=1)
    dots = jnp.sum(over_plane(pieces), axis=0)
    dots = over_z(dots)
    result1 = exchange(result1, 1)

    arrays = (q_all, k_all, near_grad, far_grad, fields, *received, near_resid, far_resid)
    rows0, rows1, rows2, rows3, own, other = last_call(
        divisor, place, sums, dots, arrays, (w_qkv.T, gain_a, lat)
    )
    late, more = over_z(own + exchange(other, 1))
    late = late + more
    late, rows1, rows2, rows3 = together(late, rows1, rows2, rows3)
    rows1, rows2, rows3 = send((rows1, rows2, rows3), (1, 2, 3))
    share = dots[0][members:] + dots[1][members:]
    own_rows = late.shape[0]
    gathered = over_plane(copies(jnp.concatenate([late, share])))
    half = jnp.concatenate(
        [
            jnp.sum(gathered[:, :own_rows], axis=0),
            gathered[:, own_rows:].reshape(-1, late.shape[1]),
        ]
    )
    other = exchange(half, 1)
    core = me % 2
    low = jnp.where(core == 0, half, other)
    high = jnp.where(core == 0, other, half)
    late = jnp.concatenate([low[:own_rows], high[:own_rows]])
    early = jnp.concatenate([low[own_rows:], high[own_rows:]])
    result = joined((result0, result1, result2, result3))
    grad_fields = joined((rows0, rows1, rows2, rows3))
    return (
        result,
        grad_fields,
        late[:channels, :channels],
        late[:channels, channels:],
        late[channels:, :channels],
        early[inner:, :channels],
        early[:inner, :channels],
        early[:inner, channels:].T,
        late[channels:, channels],
        early[inner:, channels],
    )


def solution(mesh):
    split = P("member", None, "grid")
    return jax.shard_map(
        shards,
        mesh=mesh,
        in_specs=(split, split) + (P(),) * 8,
        out_specs=(split, split) + (P(),) * 8,
        check_vma=False,
    )
```

```python
import functools

import jax
import jax.numpy as jnp
from jax import lax
from jax.experimental import pallas as pl
from jax.experimental.pallas import tpu as pltpu
from jax.sharding import PartitionSpec as P

HEADS = 4

norm_eps = 1e-05
lat_span = 1.4
sharpness_divisor = 32.0

VMEM_LIMIT = 40 * 1024 * 1024
UNROLL = 4
TOGETHER = 2
MIDDLE_UNROLL = 2
Z_PARTS = 2
f32 = jnp.float32
bf16 = jnp.bfloat16


def dot(left, right):
    return lax.dot_general(left, right, (((1,), (0,)), ((), ())), preferred_element_type=f32)


def dot_t(left, right):
    return lax.dot_general(left, right, (((1,), (1,)), ((), ())), preferred_element_type=f32)


def channel_hat(values):
    center = values - jnp.mean(values, axis=0, keepdims=True)
    spread = lax.rsqrt(jnp.mean(center * center, axis=0, keepdims=True) + norm_eps)
    return center * spread, spread


def norm_back(scaled, hat, spread):
    return spread * (
        scaled
        - jnp.mean(scaled, axis=0, keepdims=True)
        - hat * jnp.mean(scaled * hat, axis=0, keepdims=True)
    )


def member_rows(members, part):
    shape = (members * part, members)
    row = lax.broadcasted_iota(jnp.int32, shape, 0)
    column = lax.broadcasted_iota(jnp.int32, shape, 1)
    return lax.div(row, part) == column


def same_channel(members, part):
    shape = (members * part, members * part)
    row = lax.broadcasted_iota(jnp.int32, shape, 0)
    column = lax.broadcasted_iota(jnp.int32, shape, 1)
    return lax.rem(row, part) == lax.rem(column, part)


def head_rows(ref, head, part):
    members, _, cells = ref.shape
    return ref[:, head * part : (head + 1) * part, :].reshape(members * part, cells)


def pair_sums(left_ref, right_ref, out_ref):
    members, channels, _ = left_ref.shape
    part = channels // HEADS
    same = same_channel(members, part)
    collect = member_rows(members, part).astype(f32)
    sums = []
    for head in range(HEADS):
        pairs = dot_t(head_rows(left_ref, head, part), head_rows(right_ref, head, part))
        pairs = jnp.where(same, pairs, 0.0).reshape(members, part, members * part)
        lanes = jnp.sum(pairs, axis=1)
        sums.append(
            lax.dot_general(
                lanes,
                collect,
                (((1,), (0,)), ((), ())),
                precision=lax.Precision.HIGHEST,
                preferred_element_type=f32,
            )
        )
    out_ref[...] = jnp.concatenate(sums, axis=1)


def softmax_probs(score_sums, head, divisor):
    members = score_sums.shape[0]
    expo = jnp.exp(score_sums[:, head * members : (head + 1) * members] * divisor)
    return expo / jnp.sum(expo, axis=1, keepdims=True)


def per_channel(weights, spread, same, transposed):
    rows = (dot_t if transposed else dot)(spread, weights).astype(bf16)
    return jnp.where(same, dot_t(rows, spread), 0.0).astype(bf16)


def loop(count, body, unroll=UNROLL):
    def step(i, carry):
        body(i)
        return carry

    lax.fori_loop(0, count, step, 0, unroll=unroll)


def start(copies):
    for copy in copies:
        copy.start()
    return copies


def wait(copies):
    for copy in copies:
        copy.wait()


def own_cells(place, ref, width):
    return ref.at[:, :, pl.ds(pl.multiple_of(place[0] * width, width), width)]


def canonical(place, sources, target):
    block = sources[0].shape[0]
    return [
        (t, target.at[pl.ds((place[0] ^ d) * block, block)]) for d, t in enumerate(sources)
    ]


def blocks_of(*refs):
    return [ref.at[n] for ref in refs for n in range(ref.shape[0])]


def moves_of(pairs, sems, begin=0):
    return [pltpu.make_async_copy(a, b, sems.at[begin + n]) for n, (a, b) in enumerate(pairs)]


def first_kernel(distances, *refs):
    final = len(distances) == 1
    count = 1 if final else 3
    place, fields, refs = refs[0], refs[1:1 + count], refs[1 + count:]
    if final:
        before, refs = refs[:2], refs[2:]
    weights, gain, lat = refs[:3]
    outs, refs = refs[3:6], refs[6:]
    if final:
        sums, q_all, k_all, refs = refs[0], refs[1], refs[2], refs[3:]
    x, q, k, v, sin, sout = refs
    channels, cells = x.shape[2:]
    sources = list(fields)
    if not final:
        sources[0] = own_cells(place, fields[0], cells)
    block = x.shape[1]
    arrive = start(moves_of([(t, x.at[n]) for n, t in enumerate(sources)], sin))
    others = []
    if final:
        pairs = [p for t, a in zip(before, (q_all, k_all)) for p in canonical(place, blocks_of(t), a)]
        others = start(moves_of(pairs, sin, 1))
    leave = []
    for n, d in enumerate(distances):
        arrive[n].wait()

        def some(i, n=n):
            at = pl.ds(i * TOGETHER, TOGETHER)
            raw = x[n, at].astype(f32)
            center = raw - jnp.mean(raw, axis=1, keepdims=True)
            spread = lax.rsqrt(jnp.mean(center * center, axis=1, keepdims=True) + norm_eps)
            normed = (center * spread * gain[...]).astype(bf16)
            qkv = dot(weights[...], normed.reshape(TOGETHER * channels, cells))
            qkv = qkv.reshape(3, TOGETHER, channels, cells)
            q[n, at] = (qkv[0] * lat[...]).astype(bf16)
            k[n, at] = qkv[1].astype(bf16)
            v[n, at] = qkv[2].astype(bf16)

        loop(block // TOGETHER, some)
        for m, (here, there) in enumerate(zip((q, k, v), outs)):
            leave += start([pltpu.make_async_copy(here.at[n], there.at[n], sout.at[m, n])])
    if final:
        at = pl.ds((place[0] ^ distances[0]) * block, block)
        q_all[at] = q[0]
        k_all[at] = k[0]
        wait(others)
        pair_sums(q_all, k_all, sums)
    wait(leave)


def later_half(mixed, raw, grads_in, weights, result, resid_out, mixed_grad, grads):
    w_out, w_out_t, w_up, w_up_t, w_down, w_down_t, gain = weights
    g_up, g_down, g_out, g_gain = grads
    some, channels, cells = raw.shape
    flat = (some * channels, cells)

    def mean(values):
        return jnp.mean(values, axis=1, keepdims=True)

    def by_member(values):
        return values.reshape(some, -1, cells)

    def side(values):
        return jnp.concatenate([t for t in by_member(values)], axis=1)

    mixed = mixed.reshape(flat)
    grads_in = grads_in.reshape(flat)
    resid = raw.astype(f32) + by_member(dot(w_out[...], mixed))
    center = resid - mean(resid)
    spread = lax.rsqrt(mean(center * center) + norm_eps)
    hat = center * spread
    normed = (hat * gain[...]).astype(bf16).reshape(flat)
    inner = dot(w_up[...], normed)
    sig = 0.5 * jnp.tanh(0.5 * inner) + 0.5
    hidden_f = inner * sig
    hidden = hidden_f.astype(bf16)
    result[...] = (resid + by_member(dot(w_down[...], hidden))).astype(bf16)
    grad_inner = (dot(w_down_t[...], grads_in) * (sig + hidden_f * (1.0 - sig))).astype(bf16)
    grad_normed = by_member(dot(w_up_t[...], grad_inner))
    scaled = grad_normed * gain[...]
    grad_resid = by_member(grads_in.astype(f32)) + spread * (
        scaled - mean(scaled) - hat * mean(scaled * hat)
    )
    resid_out[...] = grad_resid
    grad_resid_b = grad_resid.astype(bf16).reshape(flat)
    mixed_grad[...] = by_member(dot(w_out_t[...], grad_resid_b).astype(bf16))
    g_up[...] += dot_t(side(grad_inner), side(normed))
    g_down[...] += dot_t(side(hidden), side(grads_in))
    g_out[...] += dot_t(side(grad_resid_b), side(mixed))
    g_gain[...] += jnp.sum(jnp.sum(grad_normed * hat, axis=0), axis=1, keepdims=True)


def far_kernel(divisor, *refs):
    place, sums, more_sums, v_near, v_far, x2, x3, c2, c3 = refs[:9]
    weights, refs = refs[9:16], refs[16:]
    outs, near_out, grads, refs = refs[:4], refs[4], refs[5:9], refs[9:]
    v_all, mixed_all, x, c, result, resid, grad, sin, sout = refs
    members, channels, cells = v_all.shape
    block = members // 4
    part = channels // HEADS
    values = start(moves_of(canonical(place, blocks_of(v_near, v_far), v_all), sin))
    for ref in grads:
        ref[...] = jnp.zeros_like(ref)
    spread = member_rows(members, part).astype(bf16)
    same = same_channel(members, part)
    score_sums = sums[...] + more_sums[...]
    wait(values)
    pairs = ((x2, x.at[0]), (c2, c.at[0]), (x3, x.at[1]), (c3, c.at[1]))
    arrive = start(moves_of(pairs, sin, 4))
    for head in range(HEADS):
        probs = softmax_probs(score_sums, head, divisor).astype(bf16)
        matrix = per_channel(probs, spread, same, False)
        mixed = dot(matrix, head_rows(v_all, head, part)).astype(bf16)
        mixed_all[:, head * part : (head + 1) * part, :] = mixed.reshape(members, part, cells)
    leave = start(
        [
            pltpu.make_async_copy(
                mixed_all.at[pl.ds((place[0] ^ d) * block, block)], near_out.at[d], sout.at[d]
            )
            for d in range(2)
        ]
    )
    for n in range(2):
        base = (place[0] ^ (2 + n)) * block
        wait(arrive[2 * n : 2 + 2 * n])

        def some(i, base=base, n=n):
            at = pl.ds(i * TOGETHER, TOGETHER)
            later_half(
                mixed_all[pl.ds(base + i * TOGETHER, TOGETHER)],
                x[n, at],
                c[n, at],
                weights,
                result.at[n, at],
                resid.at[n, at],
                grad.at[n, at],
                grads,
            )

        loop(block // TOGETHER, some, MIDDLE_UNROLL)
        leave += start(
            [
                pltpu.make_async_copy(result.at[n], outs[n], sout.at[2 + n]),
                pltpu.make_async_copy(resid.at[n], outs[2].at[n], sout.at[4 + n]),
                pltpu.make_async_copy(grad.at[n], outs[3].at[n], sout.at[6 + n]),
            ]
        )
    wait(leave)


def near_kernel(*refs):
    place, v_near, v_far, fields, x1, cotangent, c1, near, far_grad = refs[:9]
    weights, begun, refs = refs[9:16], refs[16:20], refs[20:]
    outs, (own, other), refs = refs[:4], refs[4:6], refs[6:]
    v_all, grad_all, mixed, x, c, result, resid, g_up, g_down, g_out, g_gain, early, sin, sout = refs
    grads = (g_up, g_down, g_out, g_gain)
    members, channels, cells = v_all.shape
    block = members // 4
    pairs = [
        (near, mixed),
        (own_cells(place, fields, cells), x.at[0]),
        (own_cells(place, cotangent, cells), c.at[0]),
        (x1, x.at[1]),
        (c1, c.at[1]),
    ]
    arrive = start(moves_of(pairs, sin))
    for ref, value in zip(grads, begun):
        ref[...] = value[...]
    arrive[0].wait()
    pairs = canonical(place, blocks_of(v_near, v_far), v_all)
    for n in range(2):
        at = pl.ds((place[0] ^ (2 + n)) * block, block)
        pairs.append((far_grad.at[n], grad_all.at[at]))
    leave = []
    for n in range(2):
        base = (place[0] ^ n) * block
        wait(arrive[1 + 2 * n : 3 + 2 * n])
        if n == 0:
            late = start(moves_of(pairs, sin, 5))

        def some(i, base=base, n=n):
            at = pl.ds(i * TOGETHER, TOGETHER)
            later_half(
                mixed[n, at],
                x[n, at],
                c[n, at],
                weights,
                result.at[n, at],
                resid.at[n, at],
                grad_all.at[pl.ds(base + i * TOGETHER, TOGETHER)],
                grads,
            )

        loop(block // TOGETHER, some, MIDDLE_UNROLL)
        leave += start(
            [
                pltpu.make_async_copy(result.at[n], outs[n], sout.at[n]),
                pltpu.make_async_copy(resid.at[n], outs[2].at[n], sout.at[2 + n]),
                pltpu.make_async_copy(
                    grad_all.at[pl.ds(base, block)], outs[3].at[n], sout.at[4 + n]
                ),
            ]
        )
    wait(late)
    pair_sums(grad_all, v_all, own.at[:members])
    wide = 2 * channels
    early[:wide, :channels] = g_up[:wide]
    early[:wide, channels:] = g_up[wide:]
    down = g_down[...].T
    early[wide : wide + channels] = down[:, :wide]
    early[wide + channels : 2 * wide] = down[:, wide:]
    early[2 * wide :, :channels] = g_out[...]
    early[2 * wide :, channels:] = jnp.broadcast_to(g_gain[...], g_out.shape).T
    half = early.shape[0] // 2
    core = lax.rem(place[0], 2)
    other[:members] = own[:members]
    own[members:] = early[pl.ds(pl.multiple_of(core * half, 8), half), :]
    other[members:] = early[pl.ds(pl.multiple_of((1 - core) * half, 8), half), :]
    wait(leave)


def last_kernel(divisor, *refs):
    place, sums, more_sums, dots, more_dots, q_near, q_far, k_near, k_far = refs[:9]
    near_grad, far_grad, fields, x1, x2, x3, near_resid, far_resid = refs[9:17]
    w_qkv_t, gain, lat = refs[17:20]
    rows_out, own, other, refs = refs[20:24], refs[24], refs[25], refs[26:]
    q_all, k_all, grad_all, x, resid, rows, qkv_all, g_qkv, g_gain, late, sin, sout = refs
    members, channels, cells = q_all.shape
    part = channels // HEADS
    block = members // 4
    keys = start(moves_of(canonical(place, blocks_of(k_near, k_far), k_all), sin))
    g_qkv[...] = jnp.zeros_like(g_qkv)
    g_gain[...] = jnp.zeros_like(g_gain)
    spread = member_rows(members, part).astype(bf16)
    same = same_channel(members, part)
    score_sums = sums[...] + more_sums[...]
    dot_sums = dots[:members] + more_dots[:members]
    probs, grad_scores = [], []
    for head in range(HEADS):
        prob = softmax_probs(score_sums, head, divisor)
        one = dot_sums[:, head * members : (head + 1) * members]
        grad_scores.append(
            (divisor * prob * (one - jnp.sum(prob * one, axis=1, keepdims=True))).astype(bf16)
        )
        probs.append(prob.astype(bf16))

    def put(offset, head, value):
        begin = offset + head * part
        qkv_all[:, begin : begin + part, :] = value.astype(bf16).reshape(members, part, cells)

    wait(keys)
    queries = start(moves_of(canonical(place, blocks_of(q_near, q_far), q_all), sin, 4))
    mixed = start(moves_of(canonical(place, blocks_of(near_grad, far_grad), grad_all), sin, 8))
    for head in range(HEADS):
        matrix = per_channel(grad_scores[head], spread, same, False)
        put(0, head, dot(matrix, head_rows(k_all, head, part)) * lat[...])
    wait(queries)
    pairs = []
    for d, source in ((2, x2), (3, x3), (1, x1), (0, own_cells(place, fields, cells))):
        pairs.append((source, x.at[d]))
        pairs.append(((near_resid if d < 2 else far_resid).at[d % 2], resid.at[d]))
    arrive = start(moves_of(pairs, sin, 12))
    for head in range(HEADS):
        matrix = per_channel(grad_scores[head], spread, same, True)
        put(channels, head, dot(matrix, head_rows(q_all, head, part)))
    wait(mixed)
    for head in range(HEADS):
        matrix = per_channel(probs[head], spread, same, True)
        put(2 * channels, head, dot(matrix, head_rows(grad_all, head, part)))

    leave = []
    for n, d in enumerate((2, 3, 1, 0)):
        base = (place[0] ^ d) * block
        wait(arrive[2 * n : 2 + 2 * n])

        def member(i, base=base, d=d):
            hat, spread = channel_hat(x[d, i].astype(f32))
            normed = (hat * gain[...]).astype(bf16)
            qkv = qkv_all[base + i]
            grad_normed = dot(w_qkv_t[...], qkv)
            rows[d, i] = (resid[d, i] + norm_back(grad_normed * gain[...], hat, spread)).astype(bf16)
            g_qkv[...] += dot_t(qkv, normed)
            g_gain[...] += jnp.sum(grad_normed * hat, axis=1, keepdims=True)

        loop(block, member)
        leave += start([pltpu.make_async_copy(rows.at[d], rows_out[d], sout.at[d])])
    late[:channels, :channels] = g_qkv[:channels]
    late[:channels, channels:] = g_qkv[channels : 2 * channels]
    late[channels:, :channels] = g_qkv[2 * channels :]
    late[channels:, channels:] = jnp.broadcast_to(g_gain[...], (channels, channels)).T
    core = lax.rem(place[0], 2)
    own[...] = late[pl.ds(pl.multiple_of(core * channels, 8), channels), :]
    other[...] = late[pl.ds(pl.multiple_of((1 - core) * channels, 8), channels), :]
    wait(leave)


def call(kernel, operands, outs, scratch, arrive, leave, microseconds):
    def spec(inside):
        return pl.BlockSpec(memory_space=pltpu.VMEM if inside else pltpu.HBM)

    place, *operands = operands
    return pl.pallas_call(
        kernel,
        in_specs=[pl.BlockSpec(memory_space=pltpu.SMEM)] + [spec(t[1]) for t in operands],
        out_specs=[spec(t[1]) for t in outs],
        out_shape=[jax.ShapeDtypeStruct(*t) if near else pltpu.HBM(*t) for t, near in outs],
        scratch_shapes=[pltpu.VMEM(*t) for t in scratch]
        + [pltpu.SemaphoreType.DMA(arrive), pltpu.SemaphoreType.DMA(leave)],
        compiler_params=pltpu.CompilerParams(vmem_limit_bytes=VMEM_LIMIT),
        cost_estimate=pl.CostEstimate(
            flops=0, bytes_accessed=microseconds * 3_600_000, transcendentals=0
        ),
    )(
        place,
        *[
            t if near else pltpu.with_memory_space_constraint(t, pltpu.HBM) for t, near in operands
        ],
    )


def inside(*arrays):
    return [(t, True) for t in arrays]


def outside(*arrays):
    return [(t, False) for t in arrays]


def first_calls(place, fields, received, weights, gain, lat):
    block, channels, cells = received[0].shape
    members = block * 4
    field = ((members, channels, cells), bf16)
    sums = ((members, HEADS * members), f32)
    three, one = (((n, block, channels, cells), bf16) for n in (3, 1))
    constants = inside(weights, gain, lat)
    before = call(
        functools.partial(first_kernel, (0, 1, 2)),
        [place] + outside(fields, *received[:2]) + constants,
        outside(three, three, three),
        [three] * 4,
        (3,),
        (3, 3),
        5,
    )
    last, *before = together(received[2], *before)
    *after, sums = call(
        functools.partial(first_kernel, (3,)),
        [place] + outside(last, *before[:2]) + constants,
        outside(one, one, one) + inside(sums),
        [field, field] + [one] * 4,
        (7,),
        (3, 1),
        5,
    )
    return list(zip(before, after)), sums, last


def far_call(divisor, place, sums, v_all, received, cots, constants):
    _, block, channels, cells = v_all[0].shape
    members = block * 4
    inner = constants[2].shape[0] // TOGETHER
    field = ((members, channels, cells), bf16)
    one = ((block, channels, cells), bf16)
    pair = ((2, block, channels, cells), bf16)
    wide = (pair[0], f32)
    grads = [((inner, channels), f32)] * 2 + [((channels, channels), f32), ((channels, 1), f32)]
    return call(
        functools.partial(far_kernel, divisor),
        [place] + inside(*sums) + outside(*v_all, *received, *cots) + inside(*constants),
        outside(one, one, wide, pair, pair) + inside(*grads),
        [field, field, pair, pair, pair, wide, pair],
        (8,),
        (8,),
        20,
    )


def near_call(place, v_all, fields, x1, cotangent, c1, near, far_grad, constants, grads):
    _, block, channels, cells = v_all[0].shape
    members = block * 4
    field = ((members, channels, cells), bf16)
    one = ((block, channels, cells), bf16)
    pair = ((2, block, channels, cells), bf16)
    wide = (pair[0], f32)
    early = grads[0].shape[0] + channels
    packed = ((members + early // 2, 2 * channels), f32)
    return call(
        near_kernel,
        [place]
        + outside(*v_all, fields, x1, cotangent, c1, near, far_grad)
        + inside(*constants, *grads),
        outside(one, one, wide, pair) + inside(packed, packed),
        [field, field, pair, pair, pair, pair, wide]
        + [(t.shape, f32) for t in grads]
        + [((early, 2 * channels), f32)],
        (11,),
        (6,),
        20,
    )


def last_call(divisor, place, sums, dots, arrays, constants):
    _, block, channels, cells = arrays[0].shape
    members = block * 4
    field = ((members, channels, cells), bf16)
    one = ((block, channels, cells), bf16)
    four = ((4, block, channels, cells), bf16)
    half = ((channels, 2 * channels), f32)
    return call(
        functools.partial(last_kernel, divisor),
        [place] + inside(*sums, *dots) + outside(*arrays) + inside(*constants),
        outside(one, one, one, one) + inside(half, half),
        [field, field, field, four, (four[0], f32), four]
        + [((members, 3 * channels, cells), bf16), ((3 * channels, channels), f32)]
        + [((channels, 1), f32), ((2 * channels, 2 * channels), f32)],
        (20,),
        (4,),
        12,
    )


def unpack_kernel(place, half, other, g_query, g_key, g_value, g_out, g_up, g_down, g_first, g_second):
    channels = g_query.shape[0]
    wide = 2 * channels
    own_is_low = lax.rem(place[0], 2) == 0
    low = jnp.where(own_is_low, half[...], other[...])
    high = jnp.where(own_is_low, other[...], half[...])
    g_query[...] = low[:channels, :channels]
    g_key[...] = low[:channels, channels:]
    g_value[...] = high[:channels, :channels]
    g_first[...] = high[:1, channels:]
    early = jnp.concatenate([low[channels:], high[channels:]])
    g_up[:wide] = early[:wide, :channels]
    g_up[wide:] = early[:wide, channels:]
    g_down[:, :wide] = early[wide : wide + channels]
    g_down[:, wide:] = early[wide + channels : 2 * wide]
    g_out[...] = early[2 * wide :, :channels]
    g_second[...] = early[2 * wide : 2 * wide + 1, channels:]


def unpack_call(place, half, other, channels, inner):
    vmem = pl.BlockSpec(memory_space=pltpu.VMEM)
    square = jax.ShapeDtypeStruct((channels, channels), f32)
    row = jax.ShapeDtypeStruct((1, channels), f32)
    return pl.pallas_call(
        unpack_kernel,
        in_specs=[pl.BlockSpec(memory_space=pltpu.SMEM), vmem, vmem],
        out_specs=[vmem] * 8,
        out_shape=[square] * 4
        + [
            jax.ShapeDtypeStruct((inner, channels), f32),
            jax.ShapeDtypeStruct((channels, inner), f32),
            row,
            row,
        ],
        compiler_params=pltpu.CompilerParams(vmem_limit_bytes=VMEM_LIMIT),
    )(place, half, other)


def exchange(array, distance, axis="member"):
    size = lax.axis_size(axis)
    return lax.ppermute(array, axis, [(i, i ^ distance) for i in range(size)])


def plane_groups():
    size = lax.axis_size("grid")
    return [list(range(part, size, Z_PARTS)) for part in range(Z_PARTS)]


def over_plane(pieces):
    return lax.all_to_all(pieces, "grid", 0, 0, axis_index_groups=plane_groups())


def copies(array):
    return jnp.broadcast_to(array[None], (lax.axis_size("grid") // Z_PARTS,) + array.shape)


def exchange_across(array):
    members, cells = lax.axis_size("member"), lax.axis_size("grid")
    pairs = [
        (m * cells + g, (m ^ 2) * cells + (g ^ 1)) for m in range(members) for g in range(cells)
    ]
    return lax.ppermute(array, ("member", "grid"), pairs)


def over_z(array):
    array = array + exchange(array, 2)
    return array, exchange_across(array)


def together(*arrays):
    return lax.optimization_barrier(arrays)


def shards(fields, cotangent, w_query, w_key, w_value, w_out, w_up, w_down, gain_attn, gain_mlp):
    block, channels, tile = fields.shape
    groups = lax.axis_size("member")
    me = lax.axis_index("member")
    width = tile // groups
    members = block * groups
    inner = w_up.shape[0]
    divisor = sharpness_divisor / ((channels // HEADS) * tile * lax.axis_size("grid"))

    def outgoing(array):
        return [
            lax.dynamic_slice_in_dim(array, (me ^ d) * width, width, axis=2) for d in range(1, groups)
        ]

    def send(pieces, distances):
        return [exchange(piece, d) for piece, d in zip(pieces, distances)]

    def joined(pieces):
        whole_tile = jnp.zeros((block, channels, tile), bf16)
        for d, piece in enumerate(pieces):
            whole_tile = lax.dynamic_update_slice_in_dim(whole_tile, piece, (me ^ d) * width, 2)
        return whole_tile

    position = (me * width).astype(f32) + jnp.arange(width, dtype=f32)
    lat = jnp.cos(lat_span * (position + 0.5) / tile)[None, :]
    w_qkv = jnp.concatenate([w_query, w_key, w_value], axis=0)
    eye = jnp.eye(TOGETHER, dtype=bf16)
    w_first = jnp.concatenate([jnp.kron(eye, t) for t in (w_query, w_key, w_value)], axis=0)
    gain_a, gain_m = gain_attn[:, None], gain_mlp[:, None]
    place = me[None].astype(jnp.int32)
    blocks = [jnp.kron(jnp.eye(TOGETHER, dtype=bf16), t) for t in (w_out, w_up, w_down)]
    constants = tuple(t for w in blocks for t in (w, w.T)) + (gain_m,)

    x1, x2, x3 = send(outgoing(fields), (1, 2, 3))
    cots = outgoing(cotangent)
    x2, x1, cots, w_first, gain_a, lat = together(x2, x1, cots, w_first, gain_a, lat)
    received = [x1, x2, x3]
    (q_all, k_all, v_all), sums, x3 = first_calls(place, fields, received, w_first, gain_a, lat)
    x3, cots = together(x3, cots)
    cots = send(cots, (1, 2, 3))

    sums = jnp.sum(over_plane(copies(sums + exchange(sums, 1))), axis=0)
    sums, cots = together(sums, cots)
    sums = over_z(sums)

    result2, result3, far_resid, far_grad, near, *begun = far_call(
        divisor, place, sums, v_all, received[1:], cots[1:], constants
    )
    result2, result3 = send((result2, result3), (2, 3))
    result0, result1, near_resid, near_grad, own, other = near_call(
        place, v_all, fields, x1, cotangent, cots[0], near, far_grad, constants, begun
    )
    own, other, result2 = together(own, other, result2)
    size = lax.axis_size("grid") // Z_PARTS
    own = own + exchange(other, 1)
    shares = own[members:].reshape(size, -1, own.shape[1])
    pieces = jnp.concatenate([copies(own[:members]), shares], axis=1)
    dots = jnp.sum(over_plane(pieces), axis=0)
    dots, result3 = together(dots, result3)
    dots = over_z(dots)
    result1 = exchange(result1, 1)

    arrays = (*q_all, *k_all, near_grad, far_grad, fields, *received, near_resid, far_resid)
    rows0, rows1, rows2, rows3, own, other = last_call(
        divisor, place, sums, dots, arrays, (w_qkv.T, gain_a, lat)
    )
    late, more = over_z(own + exchange(other, 1))
    late = late + more
    late, rows1, rows2, rows3 = together(late, rows1, rows2, rows3)
    rows1, rows2, rows3 = send((rows1, rows2, rows3), (1, 2, 3))
    share = dots[0][members:] + dots[1][members:]
    own_rows = late.shape[0]
    gathered = over_plane(copies(jnp.concatenate([late, share])))
    half = jnp.concatenate(
        [
            jnp.sum(gathered[:, :own_rows], axis=0),
            gathered[:, own_rows:].reshape(-1, late.shape[1]),
        ]
    )
    other = exchange(half, 1)
    *grads, g_gain_a, g_gain_m = unpack_call(place, half, other, channels, inner)
    result = joined((result0, result1, result2, result3))
    grad_fields = joined((rows0, rows1, rows2, rows3))
    return (result, grad_fields, *grads, g_gain_a.reshape(-1), g_gain_m.reshape(-1))


def solution(mesh):
    split = P("member", None, "grid")
    return jax.shard_map(
        shards,
        mesh=mesh,
        in_specs=(split, split) + (P(),) * 8,
        out_specs=(split, split) + (P(),) * 8,
        check_vma=False,
    )
```

```python
import functools

import jax
import jax.numpy as jnp
from jax import lax
from jax.experimental import pallas as pl
from jax.experimental.pallas import tpu as pltpu
from jax.sharding import PartitionSpec as P

HEADS = 4

norm_eps = 1e-05
lat_span = 1.4
sharpness_divisor = 32.0

VMEM_LIMIT = 40 * 1024 * 1024
UNROLL = 4
TOGETHER = 4
MIDDLE_UNROLL = 2
Z_PARTS = 2
f32 = jnp.float32
bf16 = jnp.bfloat16


def dot(left, right):
    return lax.dot_general(left, right, (((1,), (0,)), ((), ())), preferred_element_type=f32)


def dot_t(left, right):
    return lax.dot_general(left, right, (((1,), (1,)), ((), ())), preferred_element_type=f32)


def channel_hat(values):
    center = values - jnp.mean(values, axis=0, keepdims=True)
    spread = lax.rsqrt(jnp.mean(center * center, axis=0, keepdims=True) + norm_eps)
    return center * spread, spread


def norm_back(scaled, hat, spread):
    return spread * (
        scaled
        - jnp.mean(scaled, axis=0, keepdims=True)
        - hat * jnp.mean(scaled * hat, axis=0, keepdims=True)
    )


def member_rows(members, part):
    shape = (members * part, members)
    row = lax.broadcasted_iota(jnp.int32, shape, 0)
    column = lax.broadcasted_iota(jnp.int32, shape, 1)
    return lax.div(row, part) == column


def same_channel(members, part):
    shape = (members * part, members * part)
    row = lax.broadcasted_iota(jnp.int32, shape, 0)
    column = lax.broadcasted_iota(jnp.int32, shape, 1)
    return lax.rem(row, part) == lax.rem(column, part)


def head_rows(ref, head, part):
    members, _, cells = ref.shape
    return ref[:, head * part : (head + 1) * part, :].reshape(members * part, cells)


def pair_sums(left_ref, right_ref, out_ref):
    members, channels, _ = left_ref.shape
    part = channels // HEADS
    same = same_channel(members, part)
    collect = member_rows(members, part).astype(f32)
    sums = []
    for head in range(HEADS):
        pairs = dot_t(head_rows(left_ref, head, part), head_rows(right_ref, head, part))
        pairs = jnp.where(same, pairs, 0.0).reshape(members, part, members * part)
        lanes = jnp.sum(pairs, axis=1)
        sums.append(
            lax.dot_general(
                lanes,
                collect,
                (((1,), (0,)), ((), ())),
                precision=lax.Precision.HIGHEST,
                preferred_element_type=f32,
            )
        )
    out_ref[...] = jnp.concatenate(sums, axis=1)


def softmax_probs(score_sums, head, divisor):
    members = score_sums.shape[0]
    expo = jnp.exp(score_sums[:, head * members : (head + 1) * members] * divisor)
    return expo / jnp.sum(expo, axis=1, keepdims=True)


def per_channel(weights, spread, same, transposed):
    rows = (dot_t if transposed else dot)(spread, weights).astype(bf16)
    return jnp.where(same, dot_t(rows, spread), 0.0).astype(bf16)


def loop(count, body, unroll=UNROLL):
    def step(i, carry):
        body(i)
        return carry

    lax.fori_loop(0, count, step, 0, unroll=unroll)


def start(copies):
    for copy in copies:
        copy.start()
    return copies


def wait(copies):
    for copy in copies:
        copy.wait()


def own_cells(place, ref, width):
    return ref.at[:, :, pl.ds(pl.multiple_of(place[0] * width, width), width)]


def canonical(place, sources, target):
    block = sources[0].shape[0]
    return [
        (t, target.at[pl.ds((place[0] ^ d) * block, block)]) for d, t in enumerate(sources)
    ]


def blocks_of(*refs):
    return [ref.at[n] for ref in refs for n in range(ref.shape[0])]


def moves_of(pairs, sems, begin=0):
    return [pltpu.make_async_copy(a, b, sems.at[begin + n]) for n, (a, b) in enumerate(pairs)]


def first_kernel(distances, *refs):
    final = len(distances) == 1
    count = 1 if final else 3
    place, fields, refs = refs[0], refs[1:1 + count], refs[1 + count:]
    if final:
        before, refs = refs[:2], refs[2:]
    weights, gain, lat = refs[:3]
    outs, refs = refs[3:6], refs[6:]
    if final:
        sums, q_all, k_all, refs = refs[0], refs[1], refs[2], refs[3:]
    x, q, k, v, sin, sout = refs
    channels, cells = x.shape[2:]
    sources = list(fields)
    if not final:
        sources[0] = own_cells(place, fields[0], cells)
    block = x.shape[1]
    arrive = start(moves_of([(t, x.at[n]) for n, t in enumerate(sources)], sin))
    others = []
    if final:
        pairs = [p for t, a in zip(before, (q_all, k_all)) for p in canonical(place, blocks_of(t), a)]
        others = start(moves_of(pairs, sin, 1))
    leave = []
    for n, d in enumerate(distances):
        arrive[n].wait()

        def some(i, n=n):
            at = pl.ds(i * TOGETHER, TOGETHER)
            raw = x[n, at].astype(f32)
            center = raw - jnp.mean(raw, axis=1, keepdims=True)
            spread = lax.rsqrt(jnp.mean(center * center, axis=1, keepdims=True) + norm_eps)
            normed = (center * spread * gain[...]).astype(bf16)
            qkv = dot(weights[...], normed.reshape(TOGETHER * channels, cells))
            qkv = qkv.reshape(3, TOGETHER, channels, cells)
            q[n, at] = (qkv[0] * lat[...]).astype(bf16)
            k[n, at] = qkv[1].astype(bf16)
            v[n, at] = qkv[2].astype(bf16)

        loop(block // TOGETHER, some, MIDDLE_UNROLL)
        for m, (here, there) in enumerate(zip((q, k, v), outs)):
            leave += start([pltpu.make_async_copy(here.at[n], there.at[n], sout.at[m, n])])
    if final:
        at = pl.ds((place[0] ^ distances[0]) * block, block)
        q_all[at] = q[0]
        k_all[at] = k[0]
        wait(others)
        pair_sums(q_all, k_all, sums)
    wait(leave)


def later_half(mixed, raw, grads_in, weights, result, resid_out, mixed_grad, grads):
    w_out, w_out_t, w_up, w_up_t, w_down, w_down_t, gain = weights
    g_up, g_down, g_out, g_gain = grads
    some, channels, cells = raw.shape
    flat = (some * channels, cells)

    def mean(values):
        return jnp.mean(values, axis=1, keepdims=True)

    def by_member(values):
        return values.reshape(some, -1, cells)

    def side(values):
        return jnp.concatenate([t for t in by_member(values)], axis=1)

    mixed = mixed.reshape(flat)
    grads_in = grads_in.reshape(flat)
    resid = raw.astype(f32) + by_member(dot(w_out[...], mixed))
    center = resid - mean(resid)
    spread = lax.rsqrt(mean(center * center) + norm_eps)
    hat = center * spread
    normed = (hat * gain[...]).astype(bf16).reshape(flat)
    inner = dot(w_up[...], normed)
    sig = 0.5 * jnp.tanh(0.5 * inner) + 0.5
    hidden_f = inner * sig
    hidden = hidden_f.astype(bf16)
    result[...] = (resid + by_member(dot(w_down[...], hidden))).astype(bf16)
    grad_inner = (dot(w_down_t[...], grads_in) * (sig + hidden_f * (1.0 - sig))).astype(bf16)
    grad_normed = by_member(dot(w_up_t[...], grad_inner))
    scaled = grad_normed * gain[...]
    grad_resid = by_member(grads_in.astype(f32)) + spread * (
        scaled - mean(scaled) - hat * mean(scaled * hat)
    )
    resid_out[...] = grad_resid
    grad_resid_b = grad_resid.astype(bf16).reshape(flat)
    mixed_grad[...] = by_member(dot(w_out_t[...], grad_resid_b).astype(bf16))
    g_up[...] += dot_t(side(grad_inner), side(normed))
    g_down[...] += dot_t(side(hidden), side(grads_in))
    g_out[...] += dot_t(side(grad_resid_b), side(mixed))
    g_gain[...] += jnp.sum(jnp.sum(grad_normed * hat, axis=0), axis=1, keepdims=True)


def far_kernel(divisor, *refs):
    place, sums, more_sums, v_near, v_far, x2, x3, c2, c3 = refs[:9]
    weights, refs = refs[9:16], refs[16:]
    outs, near_out, grads, refs = refs[:4], refs[4], refs[5:9], refs[9:]
    v_all, mixed_all, x, c, result, resid, grad, sin, sout = refs
    members, channels, cells = v_all.shape
    block = members // 4
    part = channels // HEADS
    values = start(moves_of(canonical(place, blocks_of(v_near, v_far), v_all), sin))
    for ref in grads:
        ref[...] = jnp.zeros_like(ref)
    spread = member_rows(members, part).astype(bf16)
    same = same_channel(members, part)
    score_sums = sums[...] + more_sums[...]
    wait(values)
    pairs = ((x2, x.at[0]), (c2, c.at[0]), (x3, x.at[1]), (c3, c.at[1]))
    arrive = start(moves_of(pairs, sin, 4))
    for head in range(HEADS):
        probs = softmax_probs(score_sums, head, divisor).astype(bf16)
        matrix = per_channel(probs, spread, same, False)
        mixed = dot(matrix, head_rows(v_all, head, part)).astype(bf16)
        mixed_all[:, head * part : (head + 1) * part, :] = mixed.reshape(members, part, cells)
    leave = start(
        [
            pltpu.make_async_copy(
                mixed_all.at[pl.ds((place[0] ^ d) * block, block)], near_out.at[d], sout.at[d]
            )
            for d in range(2)
        ]
    )
    for n in range(2):
        base = (place[0] ^ (2 + n)) * block
        wait(arrive[2 * n : 2 + 2 * n])

        def some(i, base=base, n=n):
            at = pl.ds(i * TOGETHER, TOGETHER)
            later_half(
                mixed_all[pl.ds(base + i * TOGETHER, TOGETHER)],
                x[n, at],
                c[n, at],
                weights,
                result.at[n, at],
                resid.at[n, at],
                grad.at[n, at],
                grads,
            )

        loop(block // TOGETHER, some, MIDDLE_UNROLL)
        leave += start(
            [
                pltpu.make_async_copy(result.at[n], outs[n], sout.at[2 + n]),
                pltpu.make_async_copy(resid.at[n], outs[2].at[n], sout.at[4 + n]),
                pltpu.make_async_copy(grad.at[n], outs[3].at[n], sout.at[6 + n]),
            ]
        )
    wait(leave)


def near_kernel(*refs):
    place, v_near, v_far, fields, x1, cotangent, c1, near, far_grad = refs[:9]
    weights, begun, refs = refs[9:16], refs[16:20], refs[20:]
    outs, (own, other), refs = refs[:4], refs[4:6], refs[6:]
    v_all, grad_all, mixed, x, c, result, resid, g_up, g_down, g_out, g_gain, early, sin, sout = refs
    grads = (g_up, g_down, g_out, g_gain)
    members, channels, cells = v_all.shape
    block = members // 4
    pairs = [
        (near, mixed),
        (own_cells(place, fields, cells), x.at[0]),
        (own_cells(place, cotangent, cells), c.at[0]),
        (x1, x.at[1]),
        (c1, c.at[1]),
    ]
    arrive = start(moves_of(pairs, sin))
    for ref, value in zip(grads, begun):
        ref[...] = value[...]
    arrive[0].wait()
    pairs = canonical(place, blocks_of(v_near, v_far), v_all)
    for n in range(2):
        at = pl.ds((place[0] ^ (2 + n)) * block, block)
        pairs.append((far_grad.at[n], grad_all.at[at]))
    leave = []
    for n in range(2):
        base = (place[0] ^ n) * block
        wait(arrive[1 + 2 * n : 3 + 2 * n])
        if n == 0:
            late = start(moves_of(pairs, sin, 5))

        def some(i, base=base, n=n):
            at = pl.ds(i * TOGETHER, TOGETHER)
            later_half(
                mixed[n, at],
                x[n, at],
                c[n, at],
                weights,
                result.at[n, at],
                resid.at[n, at],
                grad_all.at[pl.ds(base + i * TOGETHER, TOGETHER)],
                grads,
            )

        loop(block // TOGETHER, some, MIDDLE_UNROLL)
        leave += start(
            [
                pltpu.make_async_copy(result.at[n], outs[n], sout.at[n]),
                pltpu.make_async_copy(resid.at[n], outs[2].at[n], sout.at[2 + n]),
                pltpu.make_async_copy(
                    grad_all.at[pl.ds(base, block)], outs[3].at[n], sout.at[4 + n]
                ),
            ]
        )
    wait(late)
    pair_sums(grad_all, v_all, own.at[:members])
    wide = 2 * channels
    early[:wide, :channels] = g_up[:wide]
    early[:wide, channels:] = g_up[wide:]
    down = g_down[...].T
    early[wide : wide + channels] = down[:, :wide]
    early[wide + channels : 2 * wide] = down[:, wide:]
    early[2 * wide :, :channels] = g_out[...]
    early[2 * wide :, channels:] = jnp.broadcast_to(g_gain[...], g_out.shape).T
    half = early.shape[0] // 2
    core = lax.rem(place[0], 2)
    other[:members] = own[:members]
    own[members:] = early[pl.ds(pl.multiple_of(core * half, 8), half), :]
    other[members:] = early[pl.ds(pl.multiple_of((1 - core) * half, 8), half), :]
    wait(leave)


def last_kernel(divisor, *refs):
    place, sums, more_sums, dots, more_dots, q_near, q_far, k_near, k_far = refs[:9]
    near_grad, far_grad, fields, x1, x2, x3, near_resid, far_resid = refs[9:17]
    w_qkv_t, gain, lat = refs[17:20]
    rows_out, own, other, refs = refs[20:24], refs[24], refs[25], refs[26:]
    q_all, k_all, grad_all, x, resid, rows, qkv_all, g_qkv, g_gain, late, sin, sout = refs
    members, channels, cells = q_all.shape
    part = channels // HEADS
    block = members // 4
    keys = start(moves_of(canonical(place, blocks_of(k_near, k_far), k_all), sin))
    g_qkv[...] = jnp.zeros_like(g_qkv)
    g_gain[...] = jnp.zeros_like(g_gain)
    spread = member_rows(members, part).astype(bf16)
    same = same_channel(members, part)
    score_sums = sums[...] + more_sums[...]
    dot_sums = dots[:members] + more_dots[:members]
    probs, grad_scores = [], []
    for head in range(HEADS):
        prob = softmax_probs(score_sums, head, divisor)
        one = dot_sums[:, head * members : (head + 1) * members]
        grad_scores.append(
            (divisor * prob * (one - jnp.sum(prob * one, axis=1, keepdims=True))).astype(bf16)
        )
        probs.append(prob.astype(bf16))

    def put(offset, head, value):
        begin = offset + head * part
        qkv_all[:, begin : begin + part, :] = value.astype(bf16).reshape(members, part, cells)

    wait(keys)
    queries = start(moves_of(canonical(place, blocks_of(q_near, q_far), q_all), sin, 4))
    mixed = start(moves_of(canonical(place, blocks_of(near_grad, far_grad), grad_all), sin, 8))
    for head in range(HEADS):
        matrix = per_channel(grad_scores[head], spread, same, False)
        put(0, head, dot(matrix, head_rows(k_all, head, part)) * lat[...])
    wait(queries)
    pairs = []
    for d, source in ((2, x2), (3, x3), (1, x1), (0, own_cells(place, fields, cells))):
        pairs.append((source, x.at[d]))
        pairs.append(((near_resid if d < 2 else far_resid).at[d % 2], resid.at[d]))
    arrive = start(moves_of(pairs, sin, 12))
    for head in range(HEADS):
        matrix = per_channel(grad_scores[head], spread, same, True)
        put(channels, head, dot(matrix, head_rows(q_all, head, part)))
    wait(mixed)
    for head in range(HEADS):
        matrix = per_channel(probs[head], spread, same, True)
        put(2 * channels, head, dot(matrix, head_rows(grad_all, head, part)))

    leave = []
    for n, d in enumerate((2, 3, 1, 0)):
        base = (place[0] ^ d) * block
        wait(arrive[2 * n : 2 + 2 * n])

        def member(i, base=base, d=d):
            hat, spread = channel_hat(x[d, i].astype(f32))
            normed = (hat * gain[...]).astype(bf16)
            qkv = qkv_all[base + i]
            grad_normed = dot(w_qkv_t[...], qkv)
            rows[d, i] = (resid[d, i] + norm_back(grad_normed * gain[...], hat, spread)).astype(bf16)
            g_qkv[...] += dot_t(qkv, normed)
            g_gain[...] += jnp.sum(grad_normed * hat, axis=1, keepdims=True)

        loop(block, member)
        leave += start([pltpu.make_async_copy(rows.at[d], rows_out[d], sout.at[d])])
    late[:channels, :channels] = g_qkv[:channels]
    late[:channels, channels:] = g_qkv[channels : 2 * channels]
    late[channels:, :channels] = g_qkv[2 * channels :]
    late[channels:, channels:] = jnp.broadcast_to(g_gain[...], (channels, channels)).T
    core = lax.rem(place[0], 2)
    own[...] = late[pl.ds(pl.multiple_of(core * channels, 8), channels), :]
    other[...] = late[pl.ds(pl.multiple_of((1 - core) * channels, 8), channels), :]
    wait(leave)


def call(kernel, operands, outs, scratch, arrive, leave, microseconds):
    def spec(inside):
        return pl.BlockSpec(memory_space=pltpu.VMEM if inside else pltpu.HBM)

    place, *operands = operands
    return pl.pallas_call(
        kernel,
        in_specs=[pl.BlockSpec(memory_space=pltpu.SMEM)] + [spec(t[1]) for t in operands],
        out_specs=[spec(t[1]) for t in outs],
        out_shape=[jax.ShapeDtypeStruct(*t) if near else pltpu.HBM(*t) for t, near in outs],
        scratch_shapes=[pltpu.VMEM(*t) for t in scratch]
        + [pltpu.SemaphoreType.DMA(arrive), pltpu.SemaphoreType.DMA(leave)],
        compiler_params=pltpu.CompilerParams(vmem_limit_bytes=VMEM_LIMIT),
        cost_estimate=pl.CostEstimate(
            flops=0, bytes_accessed=microseconds * 3_600_000, transcendentals=0
        ),
    )(
        place,
        *[
            t if near else pltpu.with_memory_space_constraint(t, pltpu.HBM) for t, near in operands
        ],
    )


def inside(*arrays):
    return [(t, True) for t in arrays]


def outside(*arrays):
    return [(t, False) for t in arrays]


def first_calls(place, fields, received, weights, gain, lat, cots):
    block, channels, cells = received[0].shape
    members = block * 4
    field = ((members, channels, cells), bf16)
    sums = ((members, HEADS * members), f32)
    three, one = (((n, block, channels, cells), bf16) for n in (3, 1))
    constants = inside(weights, gain, lat)
    before = call(
        functools.partial(first_kernel, (0, 1, 2)),
        [place] + outside(fields, *received[:2]) + constants,
        outside(three, three, three),
        [three] * 4,
        (3,),
        (3, 3),
        5,
    )
    before, cots = together(before, cots)
    last, *before = together(received[2], *before)
    *after, sums = call(
        functools.partial(first_kernel, (3,)),
        [place] + outside(last, *before[:2]) + constants,
        outside(one, one, one) + inside(sums),
        [field, field] + [one] * 4,
        (7,),
        (3, 1),
        5,
    )
    return list(zip(before, after)), sums, cots


def far_call(divisor, place, sums, v_all, received, cots, constants):
    _, block, channels, cells = v_all[0].shape
    members = block * 4
    inner = constants[2].shape[0] // TOGETHER
    field = ((members, channels, cells), bf16)
    one = ((block, channels, cells), bf16)
    pair = ((2, block, channels, cells), bf16)
    wide = (pair[0], f32)
    grads = [((inner, channels), f32)] * 2 + [((channels, channels), f32), ((channels, 1), f32)]
    return call(
        functools.partial(far_kernel, divisor),
        [place] + inside(*sums) + outside(*v_all, *received, *cots) + inside(*constants),
        outside(one, one, wide, pair, pair) + inside(*grads),
        [field, field, pair, pair, pair, wide, pair],
        (8,),
        (8,),
        20,
    )


def near_call(place, v_all, fields, x1, cotangent, c1, near, far_grad, constants, grads):
    _, block, channels, cells = v_all[0].shape
    members = block * 4
    field = ((members, channels, cells), bf16)
    one = ((block, channels, cells), bf16)
    pair = ((2, block, channels, cells), bf16)
    wide = (pair[0], f32)
    early = grads[0].shape[0] + channels
    packed = ((members + early // 2, 2 * channels), f32)
    return call(
        near_kernel,
        [place]
        + outside(*v_all, fields, x1, cotangent, c1, near, far_grad)
        + inside(*constants, *grads),
        outside(one, one, wide, pair) + inside(packed, packed),
        [field, field, pair, pair, pair, pair, wide]
        + [(t.shape, f32) for t in grads]
        + [((early, 2 * channels), f32)],
        (11,),
        (6,),
        20,
    )


def last_call(divisor, place, sums, dots, arrays, constants):
    _, block, channels, cells = arrays[0].shape
    members = block * 4
    field = ((members, channels, cells), bf16)
    one = ((block, channels, cells), bf16)
    four = ((4, block, channels, cells), bf16)
    half = ((channels, 2 * channels), f32)
    return call(
        functools.partial(last_kernel, divisor),
        [place] + inside(*sums, *dots) + outside(*arrays) + inside(*constants),
        outside(one, one, one, one) + inside(half, half),
        [field, field, field, four, (four[0], f32), four]
        + [((members, 3 * channels, cells), bf16), ((3 * channels, channels), f32)]
        + [((channels, 1), f32), ((2 * channels, 2 * channels), f32)],
        (20,),
        (4,),
        12,
    )


def unpack_kernel(place, half, other, g_query, g_key, g_value, g_out, g_up, g_down, g_first, g_second):
    channels = g_query.shape[0]
    wide = 2 * channels
    own_is_low = lax.rem(place[0], 2) == 0
    low = jnp.where(own_is_low, half[...], other[...])
    high = jnp.where(own_is_low, other[...], half[...])
    g_query[...] = low[:channels, :channels]
    g_key[...] = low[:channels, channels:]
    g_value[...] = high[:channels, :channels]
    g_first[...] = high[:1, channels:]
    early = jnp.concatenate([low[channels:], high[channels:]])
    g_up[:wide] = early[:wide, :channels]
    g_up[wide:] = early[:wide, channels:]
    g_down[:, :wide] = early[wide : wide + channels]
    g_down[:, wide:] = early[wide + channels : 2 * wide]
    g_out[...] = early[2 * wide :, :channels]
    g_second[...] = early[2 * wide : 2 * wide + 1, channels:]


def unpack_call(place, half, other, channels, inner):
    vmem = pl.BlockSpec(memory_space=pltpu.VMEM)
    square = jax.ShapeDtypeStruct((channels, channels), f32)
    row = jax.ShapeDtypeStruct((1, channels), f32)
    return pl.pallas_call(
        unpack_kernel,
        in_specs=[pl.BlockSpec(memory_space=pltpu.SMEM), vmem, vmem],
        out_specs=[vmem] * 8,
        out_shape=[square] * 4
        + [
            jax.ShapeDtypeStruct((inner, channels), f32),
            jax.ShapeDtypeStruct((channels, inner), f32),
            row,
            row,
        ],
        compiler_params=pltpu.CompilerParams(vmem_limit_bytes=VMEM_LIMIT),
    )(place, half, other)


def exchange(array, distance, axis="member"):
    size = lax.axis_size(axis)
    return lax.ppermute(array, axis, [(i, i ^ distance) for i in range(size)])


def plane_groups():
    size = lax.axis_size("grid")
    return [list(range(part, size, Z_PARTS)) for part in range(Z_PARTS)]


def over_plane(pieces):
    return lax.all_to_all(pieces, "grid", 0, 0, axis_index_groups=plane_groups())


def copies(array):
    return jnp.broadcast_to(array[None], (lax.axis_size("grid") // Z_PARTS,) + array.shape)


def exchange_across(array):
    members, cells = lax.axis_size("member"), lax.axis_size("grid")
    pairs = [
        (m * cells + g, (m ^ 2) * cells + (g ^ 1)) for m in range(members) for g in range(cells)
    ]
    return lax.ppermute(array, ("member", "grid"), pairs)


def over_z(array):
    beside, beyond, across = exchange(array, 2), exchange(array, 1, "grid"), exchange_across(array)
    return array + beside, beyond + across


def together(*arrays):
    return lax.optimization_barrier(arrays)


def shards(fields, cotangent, w_query, w_key, w_value, w_out, w_up, w_down, gain_attn, gain_mlp):
    block, channels, tile = fields.shape
    groups = lax.axis_size("member")
    me = lax.axis_index("member")
    width = tile // groups
    members = block * groups
    inner = w_up.shape[0]
    divisor = sharpness_divisor / ((channels // HEADS) * tile * lax.axis_size("grid"))

    def outgoing(array):
        return [
            lax.dynamic_slice_in_dim(array, (me ^ d) * width, width, axis=2) for d in range(1, groups)
        ]

    def send(pieces, distances):
        return [exchange(piece, d) for piece, d in zip(pieces, distances)]

    def joined(pieces):
        whole_tile = jnp.zeros((block, channels, tile), bf16)
        for d, piece in enumerate(pieces):
            whole_tile = lax.dynamic_update_slice_in_dim(whole_tile, piece, (me ^ d) * width, 2)
        return whole_tile

    position = (me * width).astype(f32) + jnp.arange(width, dtype=f32)
    lat = jnp.cos(lat_span * (position + 0.5) / tile)[None, :]
    w_qkv = jnp.concatenate([w_query, w_key, w_value], axis=0)
    eye = jnp.eye(TOGETHER, dtype=bf16)
    w_first = jnp.concatenate([jnp.kron(eye, t) for t in (w_query, w_key, w_value)], axis=0)
    gain_a, gain_m = gain_attn[:, None], gain_mlp[:, None]
    place = me[None].astype(jnp.int32)
    blocks = [jnp.kron(jnp.eye(TOGETHER, dtype=bf16), t) for t in (w_out, w_up, w_down)]
    constants = tuple(t for w in blocks for t in (w, w.T)) + (gain_m,)

    x1, x2, x3 = send(outgoing(fields), (1, 2, 3))
    cots = outgoing(cotangent)
    x2, x1, cots, w_first, gain_a, lat = together(x2, x1, cots, w_first, gain_a, lat)
    received = [x1, x2, x3]
    (q_all, k_all, v_all), sums, cots = first_calls(
        place, fields, received, w_first, gain_a, lat, cots
    )
    cots = send(cots, (1, 2, 3))

    sums = jnp.sum(over_plane(copies(sums + exchange(sums, 1))), axis=0)
    sums, cots = together(sums, cots)
    sums = over_z(sums)

    result2, result3, far_resid, far_grad, near, *begun = far_call(
        divisor, place, sums, v_all, received[1:], cots[1:], constants
    )
    result2, result3 = send((result2, result3), (2, 3))
    result0, result1, near_resid, near_grad, own, other = near_call(
        place, v_all, fields, x1, cotangent, cots[0], near, far_grad, constants, begun
    )
    own, other, result2 = together(own, other, result2)
    size = lax.axis_size("grid") // Z_PARTS
    own = own + exchange(other, 1)
    shares = own[members:].reshape(size, -1, own.shape[1])
    pieces = jnp.concatenate([copies(own[:members]), shares], axis=1)
    dots = jnp.sum(over_plane(pieces), axis=0)
    dots, result3 = together(dots, result3)
    dots = over_z(dots)
    result1 = exchange(result1, 1)

    arrays = (*q_all, *k_all, near_grad, far_grad, fields, *received, near_resid, far_resid)
    rows0, rows1, rows2, rows3, own, other = last_call(
        divisor, place, sums, dots, arrays, (w_qkv.T, gain_a, lat)
    )
    late, more = over_z(own + exchange(other, 1))
    late = late + more
    late, rows1, rows2, rows3 = together(late, rows1, rows2, rows3)
    rows1, rows2, rows3 = send((rows1, rows2, rows3), (1, 2, 3))
    share = dots[0][members:] + dots[1][members:]
    own_rows = late.shape[0]
    gathered = over_plane(copies(jnp.concatenate([late, share])))
    half = jnp.concatenate(
        [
            jnp.sum(gathered[:, :own_rows], axis=0),
            gathered[:, own_rows:].reshape(-1, late.shape[1]),
        ]
    )
    other = exchange(half, 1)
    *grads, g_gain_a, g_gain_m = unpack_call(place, half, other, channels, inner)
    result = joined((result0, result1, result2, result3))
    rows3, *grads = together(rows3, *grads, g_gain_a.reshape(-1), g_gain_m.reshape(-1))
    grad_fields = joined((rows0, rows1, rows2, rows3))
    return (result, grad_fields, *grads)


def solution(mesh):
    split = P("member", None, "grid")
    return jax.shard_map(
        shards,
        mesh=mesh,
        in_specs=(split, split) + (P(),) * 8,
        out_specs=(split, split) + (P(),) * 8,
        check_vma=False,
    )
```

```python
import functools

import jax
import jax.numpy as jnp
from jax import lax
from jax.experimental import pallas as pl
from jax.experimental.pallas import tpu as pltpu
from jax.sharding import PartitionSpec as P

HEADS = 4

norm_eps = 1e-05
lat_span = 1.4
sharpness_divisor = 32.0

VMEM_LIMIT = 40 * 1024 * 1024
UNROLL = 4
TOGETHER = 4
MIDDLE_UNROLL = 2
Z_PARTS = 2
f32 = jnp.float32
bf16 = jnp.bfloat16


def dot(left, right):
    return lax.dot_general(left, right, (((1,), (0,)), ((), ())), preferred_element_type=f32)


def dot_t(left, right):
    return lax.dot_general(left, right, (((1,), (1,)), ((), ())), preferred_element_type=f32)


def channel_hat(values):
    center = values - jnp.mean(values, axis=0, keepdims=True)
    spread = lax.rsqrt(jnp.mean(center * center, axis=0, keepdims=True) + norm_eps)
    return center * spread, spread


def norm_back(scaled, hat, spread):
    return spread * (
        scaled
        - jnp.mean(scaled, axis=0, keepdims=True)
        - hat * jnp.mean(scaled * hat, axis=0, keepdims=True)
    )


def member_rows(members, part):
    shape = (members * part, members)
    row = lax.broadcasted_iota(jnp.int32, shape, 0)
    column = lax.broadcasted_iota(jnp.int32, shape, 1)
    return lax.div(row, part) == column


def same_channel(members, part):
    shape = (members * part, members * part)
    row = lax.broadcasted_iota(jnp.int32, shape, 0)
    column = lax.broadcasted_iota(jnp.int32, shape, 1)
    return lax.rem(row, part) == lax.rem(column, part)


def head_rows(ref, head, part):
    members, _, cells = ref.shape
    return ref[:, head * part : (head + 1) * part, :].reshape(members * part, cells)


def pair_sums(left_ref, right_ref, out_ref):
    members, channels, _ = left_ref.shape
    part = channels // HEADS
    same = same_channel(members, part)
    collect = member_rows(members, part).astype(f32)
    sums = []
    for head in range(HEADS):
        pairs = dot_t(head_rows(left_ref, head, part), head_rows(right_ref, head, part))
        pairs = jnp.where(same, pairs, 0.0).reshape(members, part, members * part)
        lanes = jnp.sum(pairs, axis=1)
        sums.append(
            lax.dot_general(
                lanes,
                collect,
                (((1,), (0,)), ((), ())),
                precision=lax.Precision.HIGHEST,
                preferred_element_type=f32,
            )
        )
    out_ref[...] = jnp.concatenate(sums, axis=1)


def softmax_probs(score_sums, head, divisor):
    members = score_sums.shape[0]
    expo = jnp.exp(score_sums[:, head * members : (head + 1) * members] * divisor)
    return expo / jnp.sum(expo, axis=1, keepdims=True)


def per_channel(weights, spread, same, transposed):
    rows = (dot_t if transposed else dot)(spread, weights).astype(bf16)
    return jnp.where(same, dot_t(rows, spread), 0.0).astype(bf16)


def loop(count, body, unroll=UNROLL):
    def step(i, carry):
        body(i)
        return carry

    lax.fori_loop(0, count, step, 0, unroll=unroll)


def start(copies):
    for copy in copies:
        copy.start()
    return copies


def wait(copies):
    for copy in copies:
        copy.wait()


def own_cells(place, ref, width):
    return ref.at[:, :, pl.ds(pl.multiple_of(place[0] * width, width), width)]


def canonical(place, sources, target):
    block = sources[0].shape[0]
    return [
        (t, target.at[pl.ds((place[0] ^ d) * block, block)]) for d, t in enumerate(sources)
    ]


def blocks_of(*refs):
    return [ref.at[n] for ref in refs for n in range(ref.shape[0])]


def moves_of(pairs, sems, begin=0):
    return [pltpu.make_async_copy(a, b, sems.at[begin + n]) for n, (a, b) in enumerate(pairs)]


def first_kernel(distances, *refs):
    final = len(distances) == 1
    count = 1 if final else 3
    place, fields, refs = refs[0], refs[1:1 + count], refs[1 + count:]
    if final:
        before, refs = refs[:2], refs[2:]
    weights, gain, lat = refs[:3]
    outs, refs = refs[3:6], refs[6:]
    if final:
        sums, q_all, k_all, refs = refs[0], refs[1], refs[2], refs[3:]
    x, q, k, v, sin, sout = refs
    channels, cells = x.shape[2:]
    sources = list(fields)
    if not final:
        sources[0] = own_cells(place, fields[0], cells)
    block = x.shape[1]
    arrive = start(moves_of([(t, x.at[n]) for n, t in enumerate(sources)], sin))
    others = []
    if final:
        pairs = [p for t, a in zip(before, (q_all, k_all)) for p in canonical(place, blocks_of(t), a)]
        others = start(moves_of(pairs, sin, 1))
    leave = []
    for n, d in enumerate(distances):
        arrive[n].wait()

        def some(i, n=n):
            at = pl.ds(i * TOGETHER, TOGETHER)
            raw = x[n, at].astype(f32)
            center = raw - jnp.mean(raw, axis=1, keepdims=True)
            spread = lax.rsqrt(jnp.mean(center * center, axis=1, keepdims=True) + norm_eps)
            normed = (center * spread * gain[...]).astype(bf16)
            qkv = dot(weights[...], normed.reshape(TOGETHER * channels, cells))
            qkv = qkv.reshape(3, TOGETHER, channels, cells)
            q[n, at] = (qkv[0] * lat[...]).astype(bf16)
            k[n, at] = qkv[1].astype(bf16)
            v[n, at] = qkv[2].astype(bf16)

        loop(block // TOGETHER, some, MIDDLE_UNROLL)
        for m, (here, there) in enumerate(zip((q, k, v), outs)):
            leave += start([pltpu.make_async_copy(here.at[n], there.at[n], sout.at[m, n])])
    if final:
        at = pl.ds((place[0] ^ distances[0]) * block, block)
        q_all[at] = q[0]
        k_all[at] = k[0]
        wait(others)
        pair_sums(q_all, k_all, sums)
    wait(leave)


def later_half(mixed, raw, grads_in, weights, result, resid_out, mixed_grad, grads):
    w_out, w_out_t, w_up, w_up_t, w_down, w_down_t, gain = weights
    g_up, g_down, g_out, g_gain = grads
    some, channels, cells = raw.shape
    flat = (some * channels, cells)

    def mean(values):
        return jnp.mean(values, axis=1, keepdims=True)

    def by_member(values):
        return values.reshape(some, -1, cells)

    def side(values):
        return jnp.concatenate([t for t in by_member(values)], axis=1)

    mixed = mixed.reshape(flat)
    grads_in = grads_in.reshape(flat)
    resid = raw.astype(f32) + by_member(dot(w_out[...], mixed))
    center = resid - mean(resid)
    spread = lax.rsqrt(mean(center * center) + norm_eps)
    hat = center * spread
    normed = (hat * gain[...]).astype(bf16).reshape(flat)
    inner = dot(w_up[...], normed)
    sig = 0.5 * jnp.tanh(0.5 * inner) + 0.5
    hidden_f = inner * sig
    hidden = hidden_f.astype(bf16)
    result[...] = (resid + by_member(dot(w_down[...], hidden))).astype(bf16)
    grad_inner = (dot(w_down_t[...], grads_in) * (sig + hidden_f * (1.0 - sig))).astype(bf16)
    grad_normed = by_member(dot(w_up_t[...], grad_inner))
    scaled = grad_normed * gain[...]
    grad_resid = by_member(grads_in.astype(f32)) + spread * (
        scaled - mean(scaled) - hat * mean(scaled * hat)
    )
    resid_out[...] = grad_resid
    grad_resid_b = grad_resid.astype(bf16).reshape(flat)
    mixed_grad[...] = by_member(dot(w_out_t[...], grad_resid_b).astype(bf16))
    g_up[...] += dot_t(side(grad_inner), side(normed))
    g_down[...] += dot_t(side(hidden), side(grads_in))
    g_out[...] += dot_t(side(grad_resid_b), side(mixed))
    g_gain[...] += jnp.sum(jnp.sum(grad_normed * hat, axis=0), axis=1, keepdims=True)


def far_kernel(divisor, *refs):
    place, sums, more_sums, v_near, v_far, x2, x3, c2, c3 = refs[:9]
    weights, refs = refs[9:16], refs[16:]
    outs, near_out, grads, refs = refs[:4], refs[4], refs[5:9], refs[9:]
    v_all, mixed_all, x, c, result, resid, grad, sin, sout = refs
    members, channels, cells = v_all.shape
    block = members // 4
    part = channels // HEADS
    values = start(moves_of(canonical(place, blocks_of(v_near, v_far), v_all), sin))
    for ref in grads:
        ref[...] = jnp.zeros_like(ref)
    spread = member_rows(members, part).astype(bf16)
    same = same_channel(members, part)
    score_sums = sums[...] + more_sums[...]
    wait(values)
    pairs = ((x2, x.at[0]), (c2, c.at[0]), (x3, x.at[1]), (c3, c.at[1]))
    arrive = start(moves_of(pairs, sin, 4))
    for head in range(HEADS):
        probs = softmax_probs(score_sums, head, divisor).astype(bf16)
        matrix = per_channel(probs, spread, same, False)
        mixed = dot(matrix, head_rows(v_all, head, part)).astype(bf16)
        mixed_all[:, head * part : (head + 1) * part, :] = mixed.reshape(members, part, cells)
    leave = start(
        [
            pltpu.make_async_copy(
                mixed_all.at[pl.ds((place[0] ^ d) * block, block)], near_out.at[d], sout.at[d]
            )
            for d in range(2)
        ]
    )
    for n in range(2):
        base = (place[0] ^ (2 + n)) * block
        wait(arrive[2 * n : 2 + 2 * n])

        def some(i, base=base, n=n):
            at = pl.ds(i * TOGETHER, TOGETHER)
            later_half(
                mixed_all[pl.ds(base + i * TOGETHER, TOGETHER)],
                x[n, at],
                c[n, at],
                weights,
                result.at[n, at],
                resid.at[n, at],
                grad.at[n, at],
                grads,
            )

        loop(block // TOGETHER, some, MIDDLE_UNROLL)
        leave += start(
            [
                pltpu.make_async_copy(result.at[n], outs[n], sout.at[2 + n]),
                pltpu.make_async_copy(resid.at[n], outs[2].at[n], sout.at[4 + n]),
                pltpu.make_async_copy(grad.at[n], outs[3].at[n], sout.at[6 + n]),
            ]
        )
    wait(leave)


def near_kernel(*refs):
    place, v_near, v_far, fields, x1, cotangent, c1, near, far_grad = refs[:9]
    weights, begun, refs = refs[9:16], refs[16:20], refs[20:]
    outs, (own, other), refs = refs[:4], refs[4:6], refs[6:]
    v_all, grad_all, mixed, x, c, result, resid, g_up, g_down, g_out, g_gain, early, sin, sout = refs
    grads = (g_up, g_down, g_out, g_gain)
    members, channels, cells = v_all.shape
    block = members // 4
    pairs = [
        (near, mixed),
        (own_cells(place, fields, cells), x.at[0]),
        (own_cells(place, cotangent, cells), c.at[0]),
        (x1, x.at[1]),
        (c1, c.at[1]),
    ]
    arrive = start(moves_of(pairs, sin))
    for ref, value in zip(grads, begun):
        ref[...] = value[...]
    arrive[0].wait()
    pairs = canonical(place, blocks_of(v_near, v_far), v_all)
    for n in range(2):
        at = pl.ds((place[0] ^ (2 + n)) * block, block)
        pairs.append((far_grad.at[n], grad_all.at[at]))
    leave = []
    for n in range(2):
        base = (place[0] ^ n) * block
        wait(arrive[1 + 2 * n : 3 + 2 * n])
        if n == 0:
            late = start(moves_of(pairs, sin, 5))

        def some(i, base=base, n=n):
            at = pl.ds(i * TOGETHER, TOGETHER)
            later_half(
                mixed[n, at],
                x[n, at],
                c[n, at],
                weights,
                result.at[n, at],
                resid.at[n, at],
                grad_all.at[pl.ds(base + i * TOGETHER, TOGETHER)],
                grads,
            )

        loop(block // TOGETHER, some, MIDDLE_UNROLL)
        leave += start(
            [
                pltpu.make_async_copy(result.at[n], outs[n], sout.at[n]),
                pltpu.make_async_copy(resid.at[n], outs[2].at[n], sout.at[2 + n]),
                pltpu.make_async_copy(
                    grad_all.at[pl.ds(base, block)], outs[3].at[n], sout.at[4 + n]
                ),
            ]
        )
    wait(late)
    pair_sums(grad_all, v_all, own.at[:members])
    wide = 2 * channels
    early[:wide, :channels] = g_up[:wide]
    early[:wide, channels:] = g_up[wide:]
    down = g_down[...].T
    early[wide : wide + channels] = down[:, :wide]
    early[wide + channels : 2 * wide] = down[:, wide:]
    early[2 * wide :, :channels] = g_out[...]
    early[2 * wide :, channels:] = jnp.broadcast_to(g_gain[...], g_out.shape).T
    half = early.shape[0] // 2
    core = lax.rem(place[0], 2)
    other[:members] = own[:members]
    own[members:] = early[pl.ds(pl.multiple_of(core * half, 8), half), :]
    other[members:] = early[pl.ds(pl.multiple_of((1 - core) * half, 8), half), :]
    wait(leave)


def last_kernel(divisor, *refs):
    place, sums, more_sums, dots, more_dots, q_near, q_far, k_near, k_far = refs[:9]
    near_grad, far_grad, fields, x1, x2, x3, near_resid, far_resid = refs[9:17]
    w_qkv_t, gain, lat = refs[17:20]
    rows_out, own, other, refs = refs[20:24], refs[24], refs[25], refs[26:]
    q_all, k_all, grad_all, x, resid, rows, qkv_all, g_qkv, g_gain, late, sin, sout = refs
    members, channels, cells = q_all.shape
    part = channels // HEADS
    block = members // 4
    keys = start(moves_of(canonical(place, blocks_of(k_near, k_far), k_all), sin))
    g_qkv[...] = jnp.zeros_like(g_qkv)
    g_gain[...] = jnp.zeros_like(g_gain)
    spread = member_rows(members, part).astype(bf16)
    same = same_channel(members, part)
    score_sums = sums[...] + more_sums[...]
    dot_sums = dots[:members] + more_dots[:members]
    probs, grad_scores = [], []
    for head in range(HEADS):
        prob = softmax_probs(score_sums, head, divisor)
        one = dot_sums[:, head * members : (head + 1) * members]
        grad_scores.append(
            (divisor * prob * (one - jnp.sum(prob * one, axis=1, keepdims=True))).astype(bf16)
        )
        probs.append(prob.astype(bf16))

    def put(offset, head, value):
        begin = offset + head * part
        qkv_all[:, begin : begin + part, :] = value.astype(bf16).reshape(members, part, cells)

    wait(keys)
    queries = start(moves_of(canonical(place, blocks_of(q_near, q_far), q_all), sin, 4))
    mixed = start(moves_of(canonical(place, blocks_of(near_grad, far_grad), grad_all), sin, 8))
    for head in range(HEADS):
        matrix = per_channel(grad_scores[head], spread, same, False)
        put(0, head, dot(matrix, head_rows(k_all, head, part)) * lat[...])
    wait(queries)
    pairs = []
    for d, source in ((2, x2), (3, x3), (1, x1), (0, own_cells(place, fields, cells))):
        pairs.append((source, x.at[d]))
        pairs.append(((near_resid if d < 2 else far_resid).at[d % 2], resid.at[d]))
    arrive = start(moves_of(pairs, sin, 12))
    for head in range(HEADS):
        matrix = per_channel(grad_scores[head], spread, same, True)
        put(channels, head, dot(matrix, head_rows(q_all, head, part)))
    wait(mixed)
    for head in range(HEADS):
        matrix = per_channel(probs[head], spread, same, True)
        put(2 * channels, head, dot(matrix, head_rows(grad_all, head, part)))

    leave = []
    for n, d in enumerate((2, 3, 1, 0)):
        base = (place[0] ^ d) * block
        wait(arrive[2 * n : 2 + 2 * n])

        def member(i, base=base, d=d):
            hat, spread = channel_hat(x[d, i].astype(f32))
            normed = (hat * gain[...]).astype(bf16)
            qkv = qkv_all[base + i]
            grad_normed = dot(w_qkv_t[...], qkv)
            rows[d, i] = (resid[d, i] + norm_back(grad_normed * gain[...], hat, spread)).astype(bf16)
            g_qkv[...] += dot_t(qkv, normed)
            g_gain[...] += jnp.sum(grad_normed * hat, axis=1, keepdims=True)

        loop(block, member)
        leave += start([pltpu.make_async_copy(rows.at[d], rows_out[d], sout.at[d])])
    late[:channels, :channels] = g_qkv[:channels]
    late[:channels, channels:] = g_qkv[channels : 2 * channels]
    late[channels:, :channels] = g_qkv[2 * channels :]
    late[channels:, channels:] = jnp.broadcast_to(g_gain[...], (channels, channels)).T
    core = lax.rem(place[0], 2)
    own[...] = late[pl.ds(pl.multiple_of(core * channels, 8), channels), :]
    other[...] = late[pl.ds(pl.multiple_of((1 - core) * channels, 8), channels), :]
    wait(leave)


def call(kernel, operands, outs, scratch, arrive, leave, microseconds):
    def spec(inside):
        return pl.BlockSpec(memory_space=pltpu.VMEM if inside else pltpu.HBM)

    place, *operands = operands
    return pl.pallas_call(
        kernel,
        in_specs=[pl.BlockSpec(memory_space=pltpu.SMEM)] + [spec(t[1]) for t in operands],
        out_specs=[spec(t[1]) for t in outs],
        out_shape=[jax.ShapeDtypeStruct(*t) if near else pltpu.HBM(*t) for t, near in outs],
        scratch_shapes=[pltpu.VMEM(*t) for t in scratch]
        + [pltpu.SemaphoreType.DMA(arrive), pltpu.SemaphoreType.DMA(leave)],
        compiler_params=pltpu.CompilerParams(vmem_limit_bytes=VMEM_LIMIT),
        cost_estimate=pl.CostEstimate(
            flops=0, bytes_accessed=microseconds * 3_600_000, transcendentals=0
        ),
    )(
        place,
        *[
            t if near else pltpu.with_memory_space_constraint(t, pltpu.HBM) for t, near in operands
        ],
    )


def inside(*arrays):
    return [(t, True) for t in arrays]


def outside(*arrays):
    return [(t, False) for t in arrays]


def first_calls(place, fields, received, weights, gain, lat, cots):
    block, channels, cells = received[0].shape
    members = block * 4
    field = ((members, channels, cells), bf16)
    sums = ((members, HEADS * members), f32)
    three, one = (((n, block, channels, cells), bf16) for n in (3, 1))
    constants = inside(weights, gain, lat)
    before = call(
        functools.partial(first_kernel, (0, 1, 2)),
        [place] + outside(fields, *received[:2]) + constants,
        outside(three, three, three),
        [three] * 4,
        (3,),
        (3, 3),
        5,
    )
    before, cots = together(before, cots)
    last, *before = together(received[2], *before)
    *after, sums = call(
        functools.partial(first_kernel, (3,)),
        [place] + outside(last, *before[:2]) + constants,
        outside(one, one, one) + inside(sums),
        [field, field] + [one] * 4,
        (7,),
        (3, 1),
        5,
    )
    return list(zip(before, after)), sums, cots


def far_call(divisor, place, sums, v_all, received, cots, constants):
    _, block, channels, cells = v_all[0].shape
    members = block * 4
    inner = constants[2].shape[0] // TOGETHER
    field = ((members, channels, cells), bf16)
    one = ((block, channels, cells), bf16)
    pair = ((2, block, channels, cells), bf16)
    wide = (pair[0], f32)
    grads = [((inner, channels), f32)] * 2 + [((channels, channels), f32), ((channels, 1), f32)]
    return call(
        functools.partial(far_kernel, divisor),
        [place] + inside(*sums) + outside(*v_all, *received, *cots) + inside(*constants),
        outside(one, one, wide, pair, pair) + inside(*grads),
        [field, field, pair, pair, pair, wide, pair],
        (8,),
        (8,),
        20,
    )


def near_call(place, v_all, fields, x1, cotangent, c1, near, far_grad, constants, grads):
    _, block, channels, cells = v_all[0].shape
    members = block * 4
    field = ((members, channels, cells), bf16)
    one = ((block, channels, cells), bf16)
    pair = ((2, block, channels, cells), bf16)
    wide = (pair[0], f32)
    early = grads[0].shape[0] + channels
    packed = ((members + early // 2, 2 * channels), f32)
    return call(
        near_kernel,
        [place]
        + outside(*v_all, fields, x1, cotangent, c1, near, far_grad)
        + inside(*constants, *grads),
        outside(one, one, wide, pair) + inside(packed, packed),
        [field, field, pair, pair, pair, pair, wide]
        + [(t.shape, f32) for t in grads]
        + [((early, 2 * channels), f32)],
        (11,),
        (6,),
        20,
    )


def last_call(divisor, place, sums, dots, arrays, constants):
    _, block, channels, cells = arrays[0].shape
    members = block * 4
    field = ((members, channels, cells), bf16)
    one = ((block, channels, cells), bf16)
    four = ((4, block, channels, cells), bf16)
    half = ((channels, 2 * channels), f32)
    return call(
        functools.partial(last_kernel, divisor),
        [place] + inside(*sums, *dots) + outside(*arrays) + inside(*constants),
        outside(one, one, one, one) + inside(half, half),
        [field, field, field, four, (four[0], f32), four]
        + [((members, 3 * channels, cells), bf16), ((3 * channels, channels), f32)]
        + [((channels, 1), f32), ((2 * channels, 2 * channels), f32)],
        (20,),
        (4,),
        12,
    )


def unpack_kernel(place, half, other, g_query, g_key, g_value, g_out, g_up, g_down, g_first, g_second):
    channels = g_query.shape[0]
    wide = 2 * channels
    own_is_low = lax.rem(place[0], 2) == 0
    low = jnp.where(own_is_low, half[...], other[...])
    high = jnp.where(own_is_low, other[...], half[...])
    g_query[...] = low[:channels, :channels]
    g_key[...] = low[:channels, channels:]
    g_value[...] = high[:channels, :channels]
    g_first[...] = high[:1, channels:]
    early = jnp.concatenate([low[channels:], high[channels:]])
    up = early[:wide].T
    g_up[:, :wide] = up[:channels]
    g_up[:, wide:] = up[channels:]
    g_down[:, :wide] = early[wide : wide + channels]
    g_down[:, wide:] = early[wide + channels : 2 * wide]
    g_out[...] = early[2 * wide :, :channels]
    g_second[...] = early[2 * wide : 2 * wide + 1, channels:]


def place_kernel(place, piece, tile, out, sem):
    del tile
    copy = pltpu.make_async_copy(piece, own_cells(place, out, piece.shape[2]), sem)
    copy.start()
    copy.wait()


def place_call(place, piece, tile):
    hbm = pl.BlockSpec(memory_space=pltpu.HBM)
    return pl.pallas_call(
        place_kernel,
        in_specs=[
            pl.BlockSpec(memory_space=pltpu.SMEM),
            pl.BlockSpec(memory_space=pltpu.VMEM),
            hbm,
        ],
        out_specs=hbm,
        out_shape=pltpu.HBM(tile.shape, tile.dtype),
        scratch_shapes=[pltpu.SemaphoreType.DMA],
        input_output_aliases={2: 0},
        compiler_params=pltpu.CompilerParams(vmem_limit_bytes=VMEM_LIMIT),
    )(
        place,
        pltpu.with_memory_space_constraint(piece, pltpu.VMEM),
        pltpu.with_memory_space_constraint(tile, pltpu.HBM),
    )


def unpack_call(place, half, other, channels, inner):
    vmem = pl.BlockSpec(memory_space=pltpu.VMEM)
    square = jax.ShapeDtypeStruct((channels, channels), f32)
    row = jax.ShapeDtypeStruct((1, channels), f32)
    return pl.pallas_call(
        unpack_kernel,
        in_specs=[pl.BlockSpec(memory_space=pltpu.SMEM), vmem, vmem],
        out_specs=[vmem] * 8,
        out_shape=[square] * 4
        + [
            jax.ShapeDtypeStruct((channels, inner), f32),
            jax.ShapeDtypeStruct((channels, inner), f32),
            row,
            row,
        ],
        compiler_params=pltpu.CompilerParams(vmem_limit_bytes=VMEM_LIMIT),
    )(place, half, other)


def exchange(array, distance, axis="member"):
    size = lax.axis_size(axis)
    return lax.ppermute(array, axis, [(i, i ^ distance) for i in range(size)])


def plane_groups():
    size = lax.axis_size("grid")
    return [list(range(part, size, Z_PARTS)) for part in range(Z_PARTS)]


def over_plane(pieces):
    return lax.all_to_all(pieces, "grid", 0, 0, axis_index_groups=plane_groups())


def copies(array):
    return jnp.broadcast_to(array[None], (lax.axis_size("grid") // Z_PARTS,) + array.shape)


def exchange_across(array):
    members, cells = lax.axis_size("member"), lax.axis_size("grid")
    pairs = [
        (m * cells + g, (m ^ 2) * cells + (g ^ 1)) for m in range(members) for g in range(cells)
    ]
    return lax.ppermute(array, ("member", "grid"), pairs)


def over_z(array):
    beside, beyond, across = exchange(array, 2), exchange(array, 1, "grid"), exchange_across(array)
    return array + beside, beyond + across


def together(*arrays):
    return lax.optimization_barrier(arrays)


def shards(fields, cotangent, w_query, w_key, w_value, w_out, w_up, w_down, gain_attn, gain_mlp):
    block, channels, tile = fields.shape
    groups = lax.axis_size("member")
    me = lax.axis_index("member")
    width = tile // groups
    members = block * groups
    inner = w_up.shape[0]
    divisor = sharpness_divisor / ((channels // HEADS) * tile * lax.axis_size("grid"))

    def outgoing(array):
        return [
            lax.dynamic_slice_in_dim(array, (me ^ d) * width, width, axis=2) for d in range(1, groups)
        ]

    def send(pieces, distances):
        return [exchange(piece, d) for piece, d in zip(pieces, distances)]

    def joined(pieces):
        whole_tile = jnp.zeros((block, channels, tile), bf16)
        for d, piece in enumerate(pieces):
            whole_tile = lax.dynamic_update_slice_in_dim(whole_tile, piece, (me ^ d) * width, 2)
        return whole_tile

    position = (me * width).astype(f32) + jnp.arange(width, dtype=f32)
    lat = jnp.cos(lat_span * (position + 0.5) / tile)[None, :]
    w_qkv = jnp.concatenate([w_query, w_key, w_value], axis=0)
    eye = jnp.eye(TOGETHER, dtype=bf16)
    w_first = jnp.concatenate([jnp.kron(eye, t) for t in (w_query, w_key, w_value)], axis=0)
    gain_a, gain_m = gain_attn[:, None], gain_mlp[:, None]
    place = me[None].astype(jnp.int32)
    blocks = [jnp.kron(jnp.eye(TOGETHER, dtype=bf16), t) for t in (w_out, w_up, w_down)]
    constants = tuple(t for w in blocks for t in (w, w.T)) + (gain_m,)

    x1, x2, x3 = send(outgoing(fields), (1, 2, 3))
    cots = outgoing(cotangent)
    x2, x1, cots, w_first, gain_a, lat = together(x2, x1, cots, w_first, gain_a, lat)
    received = [x1, x2, x3]
    (q_all, k_all, v_all), sums, cots = first_calls(
        place, fields, received, w_first, gain_a, lat, cots
    )
    cots = send(cots, (1, 2, 3))

    sums = jnp.sum(over_plane(copies(sums + exchange(sums, 1))), axis=0)
    sums, cots = together(sums, cots)
    sums = over_z(sums)

    result2, result3, far_resid, far_grad, near, *begun = far_call(
        divisor, place, sums, v_all, received[1:], cots[1:], constants
    )
    result2, result3 = send((result2, result3), (2, 3))
    result0, result1, near_resid, near_grad, own, other = near_call(
        place, v_all, fields, x1, cotangent, cots[0], near, far_grad, constants, begun
    )
    own, other, result2 = together(own, other, result2)
    size = lax.axis_size("grid") // Z_PARTS
    own = own + exchange(other, 1)
    shares = own[members:].reshape(size, -1, own.shape[1])
    pieces = jnp.concatenate([copies(own[:members]), shares], axis=1)
    dots = jnp.sum(over_plane(pieces), axis=0)
    dots, result3 = together(dots, result3)
    dots = over_z(dots)
    result1 = exchange(result1, 1)

    arrays = (*q_all, *k_all, near_grad, far_grad, fields, *received, near_resid, far_resid)
    rows0, rows1, rows2, rows3, own, other = last_call(
        divisor, place, sums, dots, arrays, (w_qkv.T, gain_a, lat)
    )
    late, more = over_z(own + exchange(other, 1))
    late = late + more
    late, rows1, rows2, rows3 = together(late, rows1, rows2, rows3)
    rows1, rows2, rows3 = send((rows1, rows2, rows3), (1, 2, 3))
    share = dots[0][members:] + dots[1][members:]
    own_rows = late.shape[0]
    gathered = over_plane(copies(jnp.concatenate([late, share])))
    half = jnp.concatenate(
        [
            jnp.sum(gathered[:, :own_rows], axis=0),
            gathered[:, own_rows:].reshape(-1, late.shape[1]),
        ]
    )
    other = exchange(half, 1)
    *grads, g_gain_a, g_gain_m = unpack_call(place, half, other, channels, inner)
    result = joined((result0, result1, result2, result3))
    grads[4] = grads[4].T
    rows3, *grads = together(rows3, *grads, g_gain_a.reshape(-1), g_gain_m.reshape(-1))
    grad_fields = place_call(place ^ 3, rows3, joined((rows0, rows1, rows2)))
    return (result, grad_fields, *grads)


def solution(mesh):
    split = P("member", None, "grid")
    return jax.shard_map(
        shards,
        mesh=mesh,
        in_specs=(split, split) + (P(),) * 8,
        out_specs=(split, split) + (P(),) * 8,
        check_vma=False,
    )
```
